256 devices in a mesh: pole: 16 (over z, y_hi), grid: 16 (over y_lo, x, core).
Axes of the slice: x: 4, y: 4 (y_hi: 2, y_lo: 2; y = y_hi * 2 + y_lo), z: 8, core: 2. Of those that a mesh axis runs over, the one named last changes fastest.
Arguments:
- factor_cols: bfloat16 [16, 2, 3072, 1536], P('pole', None, 'grid'), may hold values from -1.1953125 to 1.1953125
- ancestor_inverse: bfloat16 [16, 2, 3072, 3072], P('pole', None, 'grid'), may hold values from -2 to 2, as said below
- pivot_inverse: float32 [16, 2, 3, 512, 512], P('pole', None, None, 'grid'), may hold values from -6 to 6
- structure: int32 [96, 3], replicated, may hold values 0 or 1
- widths: int32 [3], replicated, may hold values from 1 to 512, as said below
- pole_weights: float32 [16, 2], P('pole'), may hold values from -4 to 4
Outputs:
- column_inverse: bfloat16 [16, 2, 3072, 1536], P('pole', None, 'grid')
- pivot_block: float32 [16, 2, 3, 512, 512], P('pole', None, None, 'grid')
- density_column: float32 [3072, 1536], P('grid', 'pole')
- density_pivot: float32 [3, 512, 512], P(None, 'grid', 'pole')
The draws below stay inside these ranges and needn't reach their ends.
Inputs may be any that keep to these rules, and one draw needn't show every extreme that they name: `ancestor_inverse`: for every pole, each of the two planes is a symmetric matrix. The 3 widths sum to 768, and one of them is 512.
All inputs are finite; a program needn't handle non-finite values.
Results may differ from the reference program's by a relative error of at most 0.0004.
Values may be sent and summed in bfloat16 or wider, within the bound.
No kernel may reach another device: no remote copies, remote signals or barrier semaphores. Data moves between devices by JAX's collectives and lax.ppermute only.
A program may use at most 128 MiB of HBM per device.

```python
import math
import jax
import jax.numpy as jnp
from jax import lax

W = 512
NSUP = 3
BLK = 32
NC = 3072
COLS = 1536
NBLK = 96
POLES = 16


def draw_ancestor_inverse(key, part):
    key = jax.random.fold_in(key, 7)
    key_noise, key_sign, key_size = jax.random.split(key, 3)
    noise = jnp.clip(jax.random.normal(key_noise, (POLES, 2, NC, NC), jnp.float32), -3.0, 3.0) * (1.0 / math.sqrt(2.0 * NC))
    sym = noise + jnp.swapaxes(noise, 2, 3)
    signs = jnp.where(jax.random.bernoulli(key_sign, 0.5, (POLES, 2, NC)), 1.0, -1.0)
    sizes = jax.random.uniform(key_size, (POLES, 2, NC), jnp.float32, 1.0, 2.0)
    diagonal = signs * sizes
    ids = jnp.arange(NC, dtype=jnp.int32)
    on_diagonal = ids[:, None] == ids[None, :]
    full = jnp.where(on_diagonal[None, None], diagonal[:, :, :, None], sym)
    return full.astype(jnp.bfloat16)


def draw_widths(key, part):
    key = jax.random.fold_in(key, 11)
    key_split, key_order = jax.random.split(key, 2)
    first = jax.random.randint(key_split, (), 1, W // 2, dtype=jnp.int32)
    second = jnp.int32(W // 2) - first
    base = jnp.stack([jnp.int32(W), first, second]).astype(jnp.int32)
    order = jax.random.permutation(key_order, 3)
    return base[order].astype(jnp.int32)


def place_ends(result, own_key, smallest, top_value):
    shape = result.shape
    index_at = [jax.random.randint(jax.random.fold_in(own_key, axis), (), 0, shape[axis]) for axis in range(len(shape))]
    result = result.at[tuple(index_at)].set(smallest)
    longest = shape.index(max(shape))
    index_at[longest] = (index_at[longest] + 1) % shape[longest]
    return result.at[tuple(index_at)].set(top_value)


def block_levels(own_key, dims, cuts, least, top_value):
    def one(position, parts):
        heights = jax.random.uniform(jax.random.fold_in(jax.random.fold_in(own_key, 6), position), (parts,), jnp.float32, least / len(cuts), top_value / len(cuts))
        return jnp.repeat(jnp.exp(heights), dims[position] // parts).reshape((-1,) + (1,) * (len(dims) - position - 1))

    level = one(*cuts[0])
    for cut in cuts[1:]:
        level = level * one(*cut)
    return level


def normal_values(own_key, extent, deviation, limit, pieces=(), kind=jnp.bfloat16):
    drawn = deviation * jax.random.normal(own_key, extent, jnp.float32)
    if pieces:
        drawn = drawn * block_levels(own_key, extent, pieces, -0.22, 0.18)
    return jnp.clip(drawn, -limit, limit).astype(kind)


def setup_inputs(seed: int = 0) -> dict:
    streams_of = jax.random.split(jax.random.key(seed), 7)
    return {
        "factor_cols": normal_values(streams_of[0], (POLES, 2, NC, COLS), 0.2, 1.1953125, ((0, 16), (2, 16))),
        "ancestor_inverse": draw_ancestor_inverse(jax.random.fold_in(streams_of[6], 71), 0),
        "pivot_inverse": normal_values(streams_of[2], (POLES, 2, NSUP, W, W), 1.0, 6.0, ((0, 16), (3, 16)), jnp.float32),
        "structure": place_ends((jax.random.randint(streams_of[3], (NBLK, NSUP), 0, 2) < 1).astype(jnp.int32), jax.random.fold_in(streams_of[3], 1), 0, 1),
        "widths": draw_widths(jax.random.fold_in(streams_of[6], 71), 0),
        "pole_weights": normal_values(streams_of[5], (POLES, 2), 1.0, 4.0, ((0, 16),), jnp.float32),
    }


def reference(factor_cols, ancestor_inverse, pivot_inverse, structure, widths, pole_weights):
    row_total = factor_cols.shape[2]
    col_total = factor_cols.shape[3]
    row_blocks = jnp.arange(row_total, dtype=jnp.int32) // BLK
    row_live = structure[row_blocks].astype(jnp.float32)
    col_ids = jnp.arange(col_total, dtype=jnp.int32)
    col_sup = col_ids // W
    col_in = col_ids % W
    live_col = (col_in < widths[col_sup]).astype(jnp.float32)
    mask = row_live[:, col_sup] * live_col[None, :]
    mask_narrow = mask.astype(jnp.bfloat16)
    live_slot = (jnp.arange(W, dtype=jnp.int32)[None, :] < widths[:, None]).astype(jnp.float32)
    live_square = live_slot[:, :, None] * live_slot[:, None, :]

    def across(first, second):
        return jnp.einsum("rkc,rkd->kcd", first, second, precision=lax.Precision.HIGHEST)

    def per_pole(operands):
        factor, inverse, pivot, weight = operands
        masked = factor * mask_narrow[None]
        real_part = jnp.dot(inverse[0], masked[0], preferred_element_type=jnp.float32) - jnp.dot(inverse[1], masked[1], preferred_element_type=jnp.float32)
        imag_part = jnp.dot(inverse[0], masked[1], preferred_element_type=jnp.float32) + jnp.dot(inverse[1], masked[0], preferred_element_type=jnp.float32)
        column_full = -(jnp.stack([real_part, imag_part]) * mask[None])
        column = column_full.astype(jnp.bfloat16)
        left = masked.astype(jnp.float32).reshape(2, row_total, NSUP, W)
        right = column_full.reshape(2, row_total, NSUP, W)
        q_real = across(left[0], right[0]) - across(left[1], right[1])
        q_imag = across(left[0], right[1]) + across(left[1], right[0])
        block = (pivot - jnp.stack([q_real, q_imag])) * live_square[None]
        dens_column = weight[0] * column_full[1] + weight[1] * column_full[0]
        dens_pivot = weight[0] * block[1] + weight[1] * block[0]
        return column, block, dens_column, dens_pivot

    columns, blocks, dens_columns, dens_pivots = lax.map(per_pole, (factor_cols, ancestor_inverse, pivot_inverse, pole_weights))
    return columns, blocks, jnp.sum(dens_columns, axis=0), jnp.sum(dens_pivots, axis=0)
```

```python
import functools

import jax
import jax.numpy as jnp
from jax import lax
from jax.experimental import pallas as pl
from jax.experimental.pallas import tpu as pltpu
from jax.sharding import PartitionSpec as P

F32 = jnp.float32
BF16 = jnp.bfloat16
BIG = 512
ROWS = 192
HB = 256
HS = 128
HC = HB + HS

NX, NY, NCORE = 4, 2, 2
NZ, NH = 8, 2


def grid_perm(source):
    def at(y, x, c):
        return (y * NX + x % NX) * NCORE + c

    return [
        (at(*source(y, x, c)), at(y, x, c)) for y in range(NY) for x in range(NX) for c in range(NCORE)
    ]


def pole_perm(source):
    def at(z, h):
        return (z % NZ) * NH + h

    return [(at(*source(z, h)), at(z, h)) for z in range(NZ) for h in range(NH)]


CORE = grid_perm(lambda y, x, c: (y, x, 1 - c))
FROM_AHEAD = grid_perm(lambda y, x, c: (y, x + 1 - 2 * c, c))
FROM_BEHIND = grid_perm(lambda y, x, c: (y, x - 1 + 2 * c, c))
FROM_Y = grid_perm(lambda y, x, c: (1 - y, x, c))


def from_x(step):
    return grid_perm(lambda y, x, c: (y, x - step, c))


def from_z(step):
    return pole_perm(lambda z, h: (z - step, h))


FROM_H = pole_perm(lambda z, h: (z, 1 - h))


def place():
    g = lax.axis_index("grid")
    c = lax.rem(g, 2)
    x = lax.rem(lax.div(g, 2), NX)
    y = lax.div(g, 2 * NX)
    return g, c, x, y


def supers(widths):
    kb = jnp.where(widths[0] == BIG, 0, jnp.where(widths[1] == BIG, 1, 2))
    k1 = jnp.where(kb == 0, 1, 0)
    k2 = jnp.where(kb == 2, 1, 2)
    return kb, k1, k2, widths[k1]


def iota(shape, axis):
    return lax.broadcasted_iota(jnp.int32, shape, axis)


def row_mask(structure, block, count, k, lanes):
    return jnp.concatenate(
        [jnp.full((32, lanes), structure[block + i, k].astype(F32), F32) for i in range(count)], axis=0
    )


def call(body, outs, ins, name, flops=0, scratch=()):
    vm = pl.BlockSpec(memory_space=pltpu.VMEM)
    sm = pl.BlockSpec(memory_space=pltpu.SMEM)
    size = sum(a.size * a.dtype.itemsize for a, _ in ins) + sum(
        o.size * o.dtype.itemsize for o in outs
    )
    return pl.pallas_call(
        body,
        out_shape=tuple(outs),
        in_specs=[sm if kind == "s" else vm for _, kind in ins],
        out_specs=tuple(vm for _ in outs),
        scratch_shapes=list(scratch),
        compiler_params=pltpu.CompilerParams(vmem_limit_bytes=48 * 1024 * 1024),
        cost_estimate=pl.CostEstimate(flops=flops, bytes_accessed=size, transcendentals=0),
        name=name,
    )(*[a for a, _ in ins])


def sds(shape, dtype):
    return jax.ShapeDtypeStruct(shape, dtype)


def prep_kernel(structure, widths, f, keep, send):
    g, c, _, _ = place()
    kb, k1, k2, a = supers(widths)
    base = g * 6
    mask_b = row_mask(structure, base, 6, kb, HB).astype(BF16)
    mask_1 = row_mask(structure, base, 6, k1, HB).astype(BF16)
    mask_2 = row_mask(structure, base, 6, k2, HB).astype(BF16)
    shift = (iota((HB, HB), 0) + a == iota((HB, HB), 1)).astype(BF16)
    first = iota((ROWS, HB), 1) < a

    def at(k, part):
        return pl.ds(pl.multiple_of(k * BIG + part * HB, HB), HB)

    for p in range(2):
        o = p * HC
        keep[:, o : o + HB] = f[p, :, at(kb, c)] * mask_b
        send[:, o : o + HB] = f[p, :, at(kb, 1 - c)] * mask_b
        one = (f[p, :, at(k1, 0)] * mask_1).astype(F32)
        two = jnp.dot(f[p, :, at(k2, 0)] * mask_2, shift, preferred_element_type=F32)
        small = jnp.where(first, one, two)
        low, high = small[:, :HS], small[:, HS:]
        keep[:, o + HB : o + HC] = jnp.where(c == 0, low, high).astype(BF16)
        send[:, o + HB : o + HC] = jnp.where(c == 0, high, low).astype(BF16)


def left_kernel(widths, keep, send, got_mine, got_theirs, big, small):
    _, c, _, _ = place()
    _, _, _, a = supers(widths)
    back = (iota((HB, HB), 0) == iota((HB, HB), 1) + a).astype(BF16)
    mine = jnp.concatenate([keep[...], got_mine[...]], axis=0)
    theirs = jnp.concatenate([send[...], got_theirs[...]], axis=0)
    for p in range(2):
        o = p * HC
        big[c, p] = mine[:, o : o + HB].astype(F32).T.astype(BF16)
        big[1 - c, p] = theirs[:, o : o + HB].astype(F32).T.astype(BF16)
        m, t = mine[:, o + HB : o + HC].astype(F32), theirs[:, o + HB : o + HC].astype(F32)
        low, high = jnp.where(c == 0, m, t), jnp.where(c == 0, t, m)
        both = jnp.concatenate([low, high], axis=1)
        small[0, p] = both.T.astype(BF16)
        small[1, p] = jnp.dot(both.astype(BF16), back, preferred_element_type=F32).T.astype(BF16)


def add_blocks(get, a2s, blocks, put):
    z = None
    for a2, b in zip(a2s, blocks):
        d = jnp.dot(a2[...], b[...], preferred_element_type=F32)
        z = d if z is None else z + d
    for s in range(2):
        re, im = z[2 * s * ROWS : (2 * s + 1) * ROWS], z[(2 * s + 1) * ROWS : (2 * s + 2) * ROWS]
        old_re, old_im = get(s)
        put(s, old_re + (re[:, :HC] - im[:, HC:]), old_im + (re[:, HC:] + im[:, :HC]))


def acc_kernel(count, has_acc, *refs):
    refs = list(refs)
    old = refs.pop(0) if has_acc else None
    a2s, blocks, out = refs[:count], refs[count : 2 * count], refs[2 * count]

    def get(s):
        if old is None:
            return 0.0, 0.0
        return old[s, :, :HC], old[s, :, HC:]

    def put(s, re, im):
        out[s, :, :HC] = re
        out[s, :, HC:] = im

    add_blocks(get, a2s, blocks, put)


def column_kernel(structure, widths, old, a2, b, big, small, own, sib, q0, q1, q2, q3, gs, qb):
    g, c, x, _ = place()
    kb, k1, k2, a = supers(widths)

    def get(s):
        return old[s, :, :HC], old[s, :, HC:]

    def put(s, re, im):
        base = (g + s * (1 - 2 * c)) * 6
        mask_b = row_mask(structure, base, 6, kb, HB)
        mask_1 = row_mask(structure, base, 6, k1, HS)
        mask_2 = row_mask(structure, base, 6, k2, HS)
        mask_s = jnp.where(iota((ROWS, HS), 1) + c * HS < a, mask_1, mask_2)
        out = own if s == 0 else sib
        for p, v in ((0, re), (1, im)):
            vb = -(v[:, :HB] * mask_b)
            vs = -(v[:, HB:] * mask_s)
            out[:, p * HC : p * HC + HB] = vb
            out[:, p * HC + HB : (p + 1) * HC] = vs
            rows = slice(s * ROWS, (s + 1) * ROWS)
            for part, lo, hi in ((vb, p * HB, (p + 1) * HB), (vs, 2 * HB + p * HS, 2 * HB + (p + 1) * HS)):
                top = part.astype(BF16)
                gs[0, rows, lo:hi] = top
                gs[1, rows, lo:hi] = (part - top.astype(F32)).astype(BF16)

    add_blocks(get, [a2], [b], put)

    def across(left, lo, hi):
        return jnp.dot(left, gs[0, :, lo:hi], preferred_element_type=F32) + jnp.dot(
            left, gs[1, :, lo:hi], preferred_element_type=F32
        )

    for h in range(2):
        re = across(big[h, 0], 0, 2 * HB)
        im = across(big[h, 1], 0, 2 * HB)
        for t in range(NX):
            r = slice(64 * t, 64 * t + 64)
            qb[t, :, h * 2 * HB : h * 2 * HB + HB] = re[r, :HB] - im[r, HB:]
            qb[t, :, h * 2 * HB + HB : (h + 1) * 2 * HB] = re[r, HB:] + im[r, :HB]
    col = iota((HB, HS), 1) + c * HS
    row = iota((HB, HS), 0)
    parts = []
    for v in range(2):
        re = across(small[v, 0], 2 * HB, 2 * HB + 2 * HS)
        im = across(small[v, 1], 2 * HB, 2 * HB + 2 * HS)
        parts.append((re[:, :HS] - im[:, HS:], re[:, HS:] + im[:, :HS]))
    for p in range(2):
        e = jnp.where(
            col < a, jnp.where(row < a, parts[0][p], 0.0), jnp.where(row < HB - a, parts[1][p], 0.0)
        )
        for t in range(NX):
            qb[t, :, 4 * HB + p * HS : 4 * HB + (p + 1) * HS] = e[64 * t : 64 * t + 64]
    for d, q in enumerate((q0, q1, q2, q3)):
        q[...] = qb[lax.rem(x + d, NX)]


def spread_kernel(widths, weights, mine, other, out, *terms):
    _, c, _, _ = place()
    z = lax.div(lax.axis_index("pole"), NH)
    kb, k1, k2, a = supers(widths)
    wr, wi = weights[0, 0], weights[0, 1]
    back = (iota((HB, HB), 0) == iota((HB, HB), 1) + a).astype(BF16)
    lane = iota((ROWS, HB), 1)
    halves = []
    for ref in (mine, other):
        halves.append([(ref[:, p * HC : p * HC + HB], ref[:, p * HC + HB : (p + 1) * HC]) for p in range(2)])

    def at(k, part):
        return pl.ds(pl.multiple_of(k * BIG + part * HB, HB), HB)

    zero = jnp.zeros((ROWS, HB), BF16)
    planes = []
    for p in range(2):
        m, t = halves[0][p], halves[1][p]
        out[p, :, at(kb, c)] = m[0].astype(BF16)
        out[p, :, at(kb, 1 - c)] = t[0].astype(BF16)
        low, high = jnp.where(c == 0, m[1], t[1]), jnp.where(c == 0, t[1], m[1])
        s = jnp.concatenate([low, high], axis=1)
        sb = s.astype(BF16)
        out[p, :, at(k1, 0)] = jnp.where(lane < a, s, 0.0).astype(BF16)
        out[p, :, at(k1, 1)] = zero
        out[p, :, at(k2, 0)] = jnp.dot(sb, back, preferred_element_type=F32).astype(BF16)
        out[p, :, at(k2, 1)] = zero
        b0, b1 = jnp.where(c == 0, m[0], t[0]), jnp.where(c == 0, t[0], m[0])
        planes.append(jnp.concatenate([b0, b1, s], axis=1))
    d = wr * planes[1] + wi * planes[0]
    scratch = terms[-1]
    scratch[...] = d
    for i in range(NZ):
        to = lax.rem(z + i, NZ)
        terms[i][...] = scratch[pl.ds(pl.multiple_of(to * 24, 8), 24), :]


def fold_kernel(q0, q1, q2, q3, keep, send):
    _, _, _, y = place()
    t = q0[...] + q1[...] + q2[...] + q3[...]
    first, second, e = t[:, :BIG], t[:, BIG : 2 * BIG], t[:, 2 * BIG :]
    keep[:, :BIG] = jnp.where(y == 0, first, second)
    send[:, :BIG] = jnp.where(y == 0, second, first)
    keep[:, BIG:] = e
    send[:, BIG:] = e


def chip_kernel(keep, got, mine, send):
    _, c, _, _ = place()
    t = keep[...] + got[...]
    mine[...] = jnp.where(c == 0, t[:32], t[32:])
    send[...] = jnp.where(c == 0, t[32:], t[:32])


def pivot_kernel(widths, weights, pivot, mine, other, *rest):
    g, c, _, _ = place()
    z = lax.div(lax.axis_index("pole"), NH)
    kb, k1, k2, a = supers(widths)
    wr, wi = weights[0, 0], weights[0, 1]
    sums, out, outs, term, pay = rest[:NZ], rest[NZ], rest[NZ + 1 : 2 * NZ + 1], rest[-2], rest[-1]
    m, t = mine[...], other[...]
    row = iota((32, BIG), 0) + g * 32
    lane = iota((32, BIG), 1)
    wide = jnp.zeros((32, HB), F32)
    q = []
    for p in range(2):
        mb, tb = m[:, p * HB : (p + 1) * HB], t[:, p * HB : (p + 1) * HB]
        ms, ts = (v[:, BIG + p * HS : BIG + (p + 1) * HS] for v in (m, t))
        full = jnp.concatenate([jnp.where(c == 0, mb, tb), jnp.where(c == 0, tb, mb)], axis=1)
        e = jnp.concatenate([jnp.where(c == 0, ms, ts), jnp.where(c == 0, ts, ms)], axis=1)
        moved = pltpu.roll(e, HB - a, 1)
        q.append((full, jnp.concatenate([e, wide], axis=1), jnp.concatenate([moved, wide], axis=1)))
    for i, (k, w) in enumerate(((kb, BIG), (k1, a), (k2, HB - a))):
        live = (row < w) & (lane < w)
        blocks = []
        for p in range(2):
            v = jnp.where(live, pivot[p, k] - q[p][i], 0.0)
            out[p, k] = v
            blocks.append(v)
        term[k] = wr * blocks[1] + wi * blocks[0]
    s = sums[0][...]
    for ref in sums[1:]:
        s = s + ref[...]
    line = iota((24, HB), 1)
    small = s[:, BIG:]
    none = jnp.zeros((24, HB), F32)
    first = jnp.concatenate([jnp.where(line < a, small, 0.0), none], axis=1)
    second = jnp.concatenate(
        [jnp.where(line < HB - a, pltpu.roll(small, HB - a, 1), 0.0), none], axis=1
    )
    full = s[:, :BIG]
    slots = [
        jnp.where(kb == k, full, jnp.where(k1 == k, first, second)) for k in range(3)
    ]
    spread = jnp.concatenate(slots, axis=1)
    terms = [term[k] for k in range(3)]
    for i in range(NZ):
        pay[i, :24] = spread[:, 192 * i : 192 * (i + 1)]
        pay[i, 24:] = jnp.concatenate([v[:, 64 * i : 64 * i + 64] for v in terms], axis=1)
    for i in range(NZ):
        outs[i][...] = pay[lax.rem(z + i, NZ)]


def gather_kernel(*refs):
    pays, keep, send, all_rows = refs[:NZ], refs[NZ], refs[NZ + 1], refs[NZ + 2]
    pole = lax.axis_index("pole")
    z, h = lax.div(pole, NH), lax.rem(pole, NH)
    total = None
    for i, ref in enumerate(pays):
        source = lax.rem(z - i + NZ, NZ)
        all_rows[pl.ds(pl.multiple_of(source * 24, 8), 24), :] = ref[:24]
        total = ref[24:] if total is None else total + ref[24:]
    v = all_rows[...]
    halves = []
    for i in range(NH):
        piv = jnp.concatenate([total[:, 64 * k + 32 * i : 64 * k + 32 * i + 32] for k in range(3)], axis=1)
        halves.append((v[:, 96 * i : 96 * i + 96], piv))
    for ref, (one, two) in ((keep, (0, 1)), (send, (1, 0))):
        ref[:ROWS] = jnp.where(h == 0, halves[one][0], halves[two][0])
        ref[ROWS:] = jnp.where(h == 0, halves[one][1], halves[two][1])


def local(factor_cols, ancestor_inverse, pivot_inverse, structure, widths, pole_weights):
    g, c, x, y = place()
    side = 1 - 2 * c

    def over_grid(v, perm):
        return lax.ppermute(v, "grid", perm)

    def over_pole(v, perm):
        return lax.ppermute(v, "pole", perm)

    block = sds((ROWS, 2 * HC), BF16)
    keep, send = call(
        prep_kernel,
        [block, block],
        [(structure, "s"), (widths, "s"), (factor_cols[0], "v")],
        "prep",
        flops=2 * 2 * ROWS * HB * HB,
    )
    got_mine = over_grid(send, CORE)
    a_own = ancestor_inverse[0].reshape(2 * ROWS, -1)
    a_sib = over_grid(a_own, CORE)
    here = jnp.where(
        c == 0, jnp.concatenate([keep, got_mine], 0), jnp.concatenate([got_mine, keep], 0)
    )
    ahead = over_grid(here, FROM_AHEAD)
    behind = over_grid(here, FROM_BEHIND)
    beside = over_grid(here, FROM_Y)
    got_theirs = over_grid(keep, CORE)
    a_all = jnp.concatenate([a_own, a_sib], axis=0)

    def chip(dx, dy):
        return lax.rem(y + dy, NY) * NX + lax.rem(x + dx + NX, NX)

    def cols(at):
        return lax.dynamic_slice_in_dim(a_all, at * 2 * ROWS, 2 * ROWS, axis=1)

    def add(old, pairs):
        n = len(pairs)
        ins = ([] if old is None else [(old, "v")]) + [(cols(at), "v") for at, _ in pairs]
        ins += [(b, "v") for _, b in pairs]
        return call(
            functools.partial(acc_kernel, n, old is not None),
            [sds((2, ROWS, 2 * HC), F32)],
            ins,
            "product",
            flops=2 * n * 4 * ROWS * 2 * ROWS * 2 * HC,
        )[0]

    big, small = call(
        left_kernel,
        [sds((2, 2, HB, 2 * ROWS), BF16), sds((2, 2, HB, 2 * ROWS), BF16)],
        [(widths, "s"), (keep, "v"), (send, "v"), (got_mine, "v"), (got_theirs, "v")],
        "left",
        flops=2 * 2 * 2 * ROWS * HB * HB,
    )
    far = over_grid(ahead, FROM_AHEAD)
    beside_behind = over_grid(beside, FROM_BEHIND)
    beside_ahead = over_grid(ahead, FROM_Y)
    acc = add(
        None,
        [(chip(0, 0), here), (chip(side, 0), ahead), (chip(-side, 0), behind), (chip(0, 1), beside)],
    )
    beside_far = over_grid(beside_ahead, FROM_AHEAD)
    acc = add(
        acc,
        [(chip(2, 0), far), (chip(-side, 1), beside_behind), (chip(side, 1), beside_ahead)],
    )
    quarter = sds((64, 4 * HB + 2 * HS), F32)
    own, sib, q0, q1, q2, q3 = call(
        column_kernel,
        [sds((ROWS, 2 * HC), F32)] * 2 + [quarter] * 4,
        [
            (structure, "s"),
            (widths, "s"),
            (acc, "v"),
            (cols(chip(2, 1)), "v"),
            (beside_far, "v"),
            (big, "v"),
            (small, "v"),
        ],
        "column",
        flops=2 * 4 * ROWS * 2 * ROWS * 2 * HC + 2 * 2 * 1024 * 2 * ROWS * 768,
        scratch=[
            pltpu.VMEM((2, 2 * ROWS, 2 * HC), BF16),
            pltpu.VMEM((NX, 64, 4 * HB + 2 * HS), F32),
        ],
    )
    q1, q2, q3 = over_grid(q1, from_x(1)), over_grid(q2, from_x(2)), over_grid(q3, from_x(3))
    other = over_grid(sib, CORE)
    share = sds((24, 768), F32)
    spread = call(
        spread_kernel,
        [sds((2, ROWS, 3 * BIG), BF16)] + [share] * NZ,
        [(widths, "s"), (pole_weights, "s"), (own, "v"), (other, "v")],
        "spread",
        scratch=[pltpu.VMEM((ROWS, 768), F32)],
    )
    column_inverse, terms = spread[0], list(spread[1:])
    for i in range(1, NZ):
        terms[i] = over_pole(terms[i], from_z(i))
    rows64 = sds((64, BIG + HB), F32)
    q_keep, q_send = call(
        fold_kernel, [rows64] * 2, [(v, "v") for v in (q0, q1, q2, q3)], "fold"
    )
    q_got = over_grid(q_send, FROM_Y)
    rows32 = sds((32, BIG + HB), F32)
    p_mine, p_send = call(chip_kernel, [rows32] * 2, [(q_keep, "v"), (q_got, "v")], "chip")
    p_got = over_grid(p_send, CORE)
    pay = sds((56, 192), F32)
    pivots = call(
        pivot_kernel,
        [sds((2, 3, 32, BIG), F32)] + [pay] * NZ,
        [(widths, "s"), (pole_weights, "s"), (pivot_inverse[0], "v"), (p_mine, "v"), (p_got, "v")]
        + [(v, "v") for v in terms],
        "pivot",
        scratch=[pltpu.VMEM((3, 32, BIG), F32), pltpu.VMEM((NZ, 56, 192), F32)],
    )
    pivot_block, pays = pivots[0], list(pivots[1:])
    for i in range(1, NZ):
        pays[i] = over_pole(pays[i], from_z(i))
    last = sds((ROWS + 32, 96), F32)
    d_keep, d_send = call(
        gather_kernel,
        [last] * 2,
        [(v, "v") for v in pays],
        "slots",
        scratch=[pltpu.VMEM((ROWS, 192), F32)],
    )
    d_got = over_pole(d_send, FROM_H)
    total = d_keep + d_got
    density_column = total[:ROWS]
    density_pivot = total[ROWS:].reshape(32, 3, 32).transpose(1, 0, 2)
    return (column_inverse[None], pivot_block[None], density_column, density_pivot)


def solution(mesh):
    in_specs = (
        P("pole", None, "grid", None),
        P("pole", None, "grid", None),
        P("pole", None, None, "grid", None),
        P(),
        P(),
        P("pole", None),
    )
    out_specs = (
        P("pole", None, "grid", None),
        P("pole", None, None, "grid", None),
        P("grid", "pole"),
        P(None, "grid", "pole"),
    )
    return jax.shard_map(local, mesh=mesh, in_specs=in_specs, out_specs=out_specs, check_vma=False)
```

```python
import functools

import jax
import jax.numpy as jnp
from jax import lax
from jax.experimental import pallas as pl
from jax.experimental.pallas import tpu as pltpu
from jax.sharding import PartitionSpec as P

F32 = jnp.float32
BF16 = jnp.bfloat16
BIG = 512
ROWS = 192
HB = 256
HS = 128
HC = HB + HS

NX, NY, NCORE = 4, 2, 2
NZ, NH = 8, 2


def grid_perm(source):
    def at(y, x, c):
        return (y * NX + x % NX) * NCORE + c

    return [
        (at(*source(y, x, c)), at(y, x, c)) for y in range(NY) for x in range(NX) for c in range(NCORE)
    ]


CORE = grid_perm(lambda y, x, c: (y, x, 1 - c))
FROM_AHEAD = grid_perm(lambda y, x, c: (y, x + 1 - 2 * c, c))
FROM_BEHIND = grid_perm(lambda y, x, c: (y, x - 1 + 2 * c, c))
FROM_Y = grid_perm(lambda y, x, c: (1 - y, x, c))


def pole_perm(source):
    def at(z, h):
        return z * NH + h

    return [(at(*source(z, h)), at(z, h)) for z in range(NZ) for h in range(NH)]


Z_PAIR = pole_perm(lambda z, h: (z ^ 1, h))
Z_GROUPS = [[z * NH + h for z in range(b, NZ, 2) for h in range(NH)] for b in range(2)]


def place():
    g = lax.axis_index("grid")
    c = lax.rem(g, 2)
    x = lax.rem(lax.div(g, 2), NX)
    y = lax.div(g, 2 * NX)
    return g, c, x, y


def parity():
    return lax.rem(lax.div(lax.axis_index("pole"), NH), 2)


def slot(i, bit):
    return 4 * (i // 2) + 2 * bit + i % 2


def supers(widths):
    kb = jnp.where(widths[0] == BIG, 0, jnp.where(widths[1] == BIG, 1, 2))
    k1 = jnp.where(kb == 0, 1, 0)
    k2 = jnp.where(kb == 2, 1, 2)
    return kb, k1, k2, widths[k1]


def iota(shape, axis):
    return lax.broadcasted_iota(jnp.int32, shape, axis)


def row_mask(structure, block, count, k, lanes):
    return jnp.concatenate(
        [jnp.full((32, lanes), structure[block + i, k].astype(F32), F32) for i in range(count)], axis=0
    )


def call(body, outs, ins, name, flops=0, scratch=(), blocks=None, limit=16, out_space=pltpu.VMEM):
    specs = []
    for a, kind in ins:
        if kind == "s":
            specs.append(pl.BlockSpec(memory_space=pltpu.SMEM))
        elif kind == "v":
            specs.append(pl.BlockSpec(memory_space=pltpu.VMEM))
        else:
            specs.append(pl.BlockSpec((a.shape[0], 2 * ROWS), lambda i, at, n=kind[0]: (0, at[n])))
    size = sum(a.size * a.dtype.itemsize for a, kind in ins if kind in ("s", "v")) + sum(
        o.size * o.dtype.itemsize for o in outs
    )
    common = dict(
        out_shape=tuple(pltpu.HBM(o.shape, o.dtype) for o in outs) if out_space is pltpu.HBM else tuple(outs),
        compiler_params=pltpu.CompilerParams(vmem_limit_bytes=limit * 1024 * 1024),
        cost_estimate=pl.CostEstimate(flops=flops, bytes_accessed=size, transcendentals=0),
        name=name,
    )
    out_specs = tuple(pl.BlockSpec(memory_space=out_space) for _ in outs)
    operands = [a for a, _ in ins]
    if blocks is None:
        return pl.pallas_call(
            body, in_specs=specs, out_specs=out_specs, scratch_shapes=list(scratch), **common
        )(*operands)
    grid_spec = pltpu.PrefetchScalarGridSpec(
        num_scalar_prefetch=1,
        grid=(1,),
        in_specs=specs,
        out_specs=out_specs,
        scratch_shapes=list(scratch),
    )
    return pl.pallas_call(body, grid_spec=grid_spec, **common)(jnp.stack(blocks), *operands)


def sds(shape, dtype):
    return jax.ShapeDtypeStruct(shape, dtype)


def prep_kernel(structure, widths, f, keep, send):
    g, c, _, _ = place()
    kb, k1, k2, a = supers(widths)
    base = g * 6
    mask_b = row_mask(structure, base, 6, kb, HB).astype(BF16)
    mask_1 = row_mask(structure, base, 6, k1, HB).astype(BF16)
    mask_2 = row_mask(structure, base, 6, k2, HB).astype(BF16)
    shift = (iota((HB, HB), 0) + a == iota((HB, HB), 1)).astype(BF16)
    first = iota((ROWS, HB), 1) < a

    def at(k, part):
        return pl.ds(pl.multiple_of(k * BIG + part * HB, HB), HB)

    for p in range(2):
        o = p * HC
        keep[:, o : o + HB] = f[p, :, at(kb, c)] * mask_b
        send[:, o : o + HB] = f[p, :, at(kb, 1 - c)] * mask_b
        one = (f[p, :, at(k1, 0)] * mask_1).astype(F32)
        two = jnp.dot(f[p, :, at(k2, 0)] * mask_2, shift, preferred_element_type=F32)
        small = jnp.where(first, one, two)
        low, high = small[:, :HS], small[:, HS:]
        keep[:, o + HB : o + HC] = jnp.where(c == 0, low, high).astype(BF16)
        send[:, o + HB : o + HC] = jnp.where(c == 0, high, low).astype(BF16)


def left_kernel(widths, keep, send, got_mine, got_theirs, big, small):
    _, c, _, _ = place()
    _, _, _, a = supers(widths)
    back = (iota((HB, HB), 0) == iota((HB, HB), 1) + a).astype(BF16)
    mine = jnp.concatenate([keep[...], got_mine[...]], axis=0)
    theirs = jnp.concatenate([send[...], got_theirs[...]], axis=0)
    for p in range(2):
        o = p * HC
        big[c, p] = mine[:, o : o + HB].astype(F32).T.astype(BF16)
        big[1 - c, p] = theirs[:, o : o + HB].astype(F32).T.astype(BF16)
        m, t = mine[:, o + HB : o + HC].astype(F32), theirs[:, o + HB : o + HC].astype(F32)
        low, high = jnp.where(c == 0, m, t), jnp.where(c == 0, t, m)
        both = jnp.concatenate([low, high], axis=1)
        small[0, p] = both.T.astype(BF16)
        small[1, p] = jnp.dot(both.astype(BF16), back, preferred_element_type=F32).T.astype(BF16)


def add_blocks(get, a_own, a_sib, us, vs, put, rows):
    _, c, _, _ = place()
    for i, (u, v) in enumerate(zip(us, vs)):
        for part, ref in ((c, u), (1 - c, v)):
            rows[pl.ds(pl.multiple_of((2 * i + part) * ROWS, ROWS), ROWS), :] = ref[...]
    for s, refs in enumerate((a_own, a_sib)):
        left = jnp.concatenate([ref[...] for ref in refs], axis=1)
        z = jnp.dot(left, rows[...], preferred_element_type=F32)
        re, im = z[:ROWS], z[ROWS:]
        old_re, old_im = get(s)
        put(s, old_re + (re[:, :HC] - im[:, HC:]), old_im + (re[:, HC:] + im[:, :HC]))


def acc_kernel(count, has_acc, *refs):
    refs = list(refs[1:])
    old = refs.pop(0) if has_acc else None
    a_own, a_sib, us, vs = (refs[i * count : (i + 1) * count] for i in range(4))
    out, rows = refs[4 * count :]

    def get(s):
        if old is None:
            return 0.0, 0.0
        return old[s, :, :HC], old[s, :, HC:]

    def put(s, re, im):
        out[s, :, :HC] = re
        out[s, :, HC:] = im

    add_blocks(get, a_own, a_sib, us, vs, put, rows)


def column_kernel(_, structure, widths, old, a_own, a_sib, u, v, big, small, own_out, sib_out, q_out, rows, gs, own, sib, q, sems):
    g, c, _, _ = place()
    kb, k1, k2, a = supers(widths)

    def get(s):
        return old[s, :, :HC], old[s, :, HC:]

    def put(s, re, im):
        base = (g + s * (1 - 2 * c)) * 6
        mask_b = row_mask(structure, base, 6, kb, HB)
        mask_1 = row_mask(structure, base, 6, k1, HS)
        mask_2 = row_mask(structure, base, 6, k2, HS)
        mask_s = jnp.where(iota((ROWS, HS), 1) + c * HS < a, mask_1, mask_2)
        out = own if s == 0 else sib
        for p, w in ((0, re), (1, im)):
            vb = -(w[:, :HB] * mask_b)
            vs = -(w[:, HB:] * mask_s)
            out[:, p * HC : p * HC + HB] = vb
            out[:, p * HC + HB : (p + 1) * HC] = vs
            at = slice(s * ROWS, (s + 1) * ROWS)
            for part, lo, hi in ((vb, p * HB, (p + 1) * HB), (vs, 2 * HB + p * HS, 2 * HB + (p + 1) * HS)):
                top = part.astype(BF16)
                gs[0, at, lo:hi] = top
                gs[1, at, lo:hi] = (part - top.astype(F32)).astype(BF16)

    add_blocks(get, [a_own], [a_sib], [u], [v], put, rows)
    copies = [pltpu.make_async_copy(sib, sib_out, sems.at[0]), pltpu.make_async_copy(own, own_out, sems.at[1])]
    for copy in copies:
        copy.start()

    def across(left, lo, hi):
        return jnp.dot(left, gs[0, :, lo:hi], preferred_element_type=F32) + jnp.dot(
            left, gs[1, :, lo:hi], preferred_element_type=F32
        )

    for h in range(2):
        re = across(big[h, 0], 0, 2 * HB)
        im = across(big[h, 1], 0, 2 * HB)
        for t in range(8):
            r = slice(32 * t, 32 * t + 32)
            q[8 * h + t, :, :HB] = re[r, :HB] - im[r, HB:]
            q[8 * h + t, :, HB:BIG] = re[r, HB:] + im[r, :HB]
    col = iota((HB, HS), 1) + c * HS
    row = iota((HB, HS), 0)
    parts = []
    for i in range(2):
        re = across(small[i, 0], 2 * HB, 2 * HB + 2 * HS)
        im = across(small[i, 1], 2 * HB, 2 * HB + 2 * HS)
        parts.append((re[:, :HS] - im[:, HS:], re[:, HS:] + im[:, :HS]))
    for p in range(2):
        e = jnp.where(
            col < a, jnp.where(row < a, parts[0][p], 0.0), jnp.where(row < HB - a, parts[1][p], 0.0)
        )
        at = slice(BIG + p * HS, BIG + (p + 1) * HS)
        for t in range(8):
            q[t, :, at] = e[32 * t : 32 * t + 32]
            q[8 + t, :, at] = jnp.zeros((32, HS), F32)
    copies.append(pltpu.make_async_copy(q, q_out, sems.at[2]))
    copies[2].start()
    for copy in copies:
        copy.wait()


def spread_kernel(widths, weights, mine, other, out, keep, send, wide):
    _, c, _, _ = place()
    odd = parity()
    kb, k1, k2, a = supers(widths)
    wr, wi = weights[0, 0], weights[0, 1]
    back = (iota((HB, HB), 0) == iota((HB, HB), 1) + a).astype(BF16)
    lane = iota((ROWS, HB), 1)
    halves = []
    for ref in (mine, other):
        halves.append([(ref[:, p * HC : p * HC + HB], ref[:, p * HC + HB : (p + 1) * HC]) for p in range(2)])

    def at(k, part):
        return pl.ds(pl.multiple_of(k * BIG + part * HB, HB), HB)

    zero = jnp.zeros((ROWS, HB), BF16)
    small = []
    for p in range(2):
        m, t = halves[0][p], halves[1][p]
        out[p, :, at(kb, c)] = m[0].astype(BF16)
        out[p, :, at(kb, 1 - c)] = t[0].astype(BF16)
        low, high = jnp.where(c == 0, m[1], t[1]), jnp.where(c == 0, t[1], m[1])
        s = jnp.concatenate([low, high], axis=1)
        sb = s.astype(BF16)
        out[p, :, at(k1, 0)] = jnp.where(lane < a, s, 0.0).astype(BF16)
        out[p, :, at(k1, 1)] = zero
        out[p, :, at(k2, 0)] = jnp.dot(sb, back, preferred_element_type=F32).astype(BF16)
        out[p, :, at(k2, 1)] = zero
        small.append(s)
    for i, part in ((0, c), (1, 1 - c)):
        wide[:, at(kb, part)] = wr * halves[i][1][0] + wi * halves[i][0][0]
    d = wr * small[1] + wi * small[0]
    none = jnp.zeros((ROWS, HB), F32)
    wide[:, at(k1, 0)] = jnp.where(lane < a, d, 0.0)
    wide[:, at(k1, 1)] = none
    wide[:, at(k2, 0)] = jnp.where(lane < HB - a, pltpu.roll(d, HB - a, 1), 0.0)
    wide[:, at(k2, 1)] = none
    v = wide[...]
    for j in range(8):
        parts = [
            jnp.concatenate([v[48 * i : 48 * i + 48, 96 * p : 96 * p + 96] for i in range(4)], axis=1)
            for p in (slot(j, 0), slot(j, 1))
        ]
        keep[j] = jnp.where(odd == 0, parts[0], parts[1])
        send[j] = jnp.where(odd == 0, parts[1], parts[0])


def pivot_kernel(widths, weights, pivot, sums, keep, got, block, pay, wide):
    g = lax.axis_index("grid")
    kb, k1, k2, a = supers(widths)
    wr, wi = weights[0, 0], weights[0, 1]
    m, t = sums[0], sums[1]
    for i in range(1, 8):
        m, t = m + sums[2 * i], t + sums[2 * i + 1]
    row = iota((32, BIG), 0) + g * 32
    line = iota((32, BIG), 1)
    blank = jnp.zeros((32, HB), F32)
    q = []
    for p in range(2):
        full = jnp.concatenate([u[:, p * HB : (p + 1) * HB] for u in (m, t)], axis=1)
        e = jnp.concatenate([u[:, BIG + p * HS : BIG + (p + 1) * HS] for u in (m, t)], axis=1)
        moved = pltpu.roll(e, HB - a, 1)
        q.append((full, jnp.concatenate([e, blank], axis=1), jnp.concatenate([moved, blank], axis=1)))
    for i, (k, w) in enumerate(((kb, BIG), (k1, a), (k2, HB - a))):
        live = (row < w) & (line < w)
        blocks = []
        for p in range(2):
            b = jnp.where(live, pivot[p, k] - q[p][i], 0.0)
            block[p, k] = b
            blocks.append(b)
        wide[pl.ds(pl.multiple_of(k * 32, 32), 32), :] = wr * blocks[1] + wi * blocks[0]
    v = wide[...]
    for j in range(8):
        pay[j, :48] = keep[j] + got[j]
        for bit in range(2):
            p = slot(j, bit)
            pay[j, 48 + 8 * bit : 56 + 8 * bit] = jnp.concatenate(
                [v[8 * i : 8 * i + 8, 32 * p : 32 * p + 32] for i in range(12)], axis=1
            )


def density_kernel(pays, column, keep, send):
    odd = parity()
    v = pays[0]
    for i in range(1, 8):
        v = v + pays[i]
    for i in range(4):
        column[48 * i : 48 * i + 48] = v[:48, 96 * i : 96 * i + 96]
    keep[...] = jnp.where(odd == 0, v[48:56], v[56:])
    send[...] = jnp.where(odd == 0, v[56:], v[48:56])


def last_kernel(keep, got, pivot):
    v = keep[...] + got[...]
    for i in range(12):
        pivot[i // 4, 8 * (i % 4) : 8 * (i % 4) + 8] = v[:, 32 * i : 32 * i + 32]


def local(factor_cols, ancestor_inverse, pivot_inverse, structure, widths, pole_weights):
    g, c, x, y = place()
    side = 1 - 2 * c

    def over_grid(v, perm):
        return lax.ppermute(v, "grid", perm)

    block = sds((ROWS, 2 * HC), BF16)
    keep, send = call(
        prep_kernel,
        [block, block],
        [(structure, "s"), (widths, "s"), (factor_cols[0], "v")],
        "prep",
        flops=2 * 2 * ROWS * HB * HB,
    )
    a_own = ancestor_inverse[0].reshape(2 * ROWS, -1)
    a_sib = over_grid(a_own, CORE)
    keep, send, a_sib = lax.optimization_barrier((keep, send, a_sib))
    got_mine, got_theirs = over_grid(send, CORE), over_grid(keep, CORE)
    got_mine, got_theirs = lax.optimization_barrier((got_mine, got_theirs))

    def chip(dx, dy):
        return lax.rem(y + dy, NY) * NX + lax.rem(x + dx + NX, NX)

    def first(v):
        return [over_grid(v, perm) for perm in (FROM_AHEAD, FROM_BEHIND, FROM_Y)]

    def second(ahead, behind, beside):
        return [over_grid(ahead, FROM_AHEAD), over_grid(beside, FROM_BEHIND), over_grid(ahead, FROM_Y)]

    def add(old, places, us, vs):
        n = len(places)
        ins = ([] if old is None else [(old, "v")]) + [(a, (i,)) for a in (a_own, a_sib) for i in range(n)]
        ins += [(b, "v") for b in (*us, *vs)]
        return call(
            functools.partial(acc_kernel, n, old is not None),
            [sds((2, ROWS, 2 * HC), F32)],
            ins,
            "product",
            flops=2 * n * 4 * ROWS * 2 * ROWS * 2 * HC,
            scratch=[pltpu.VMEM((n * 2 * ROWS, 2 * HC), BF16)],
            blocks=places,
        )[0]

    v1 = first(got_mine)
    u1 = first(keep)
    v2 = second(*v1)
    acc = add(None, [chip(0, 0)], [keep], [got_mine])
    big, small = call(
        left_kernel,
        [sds((2, 2, HB, 2 * ROWS), BF16), sds((2, 2, HB, 2 * ROWS), BF16)],
        [(widths, "s"), (keep, "v"), (send, "v"), (got_mine, "v"), (got_theirs, "v")],
        "left",
        flops=2 * 2 * 2 * ROWS * HB * HB,
    )
    *u1, acc, big, small = lax.optimization_barrier((*u1, acc, big, small))
    u2 = second(*u1)
    acc = add(acc, [chip(side, 0), chip(-side, 0), chip(0, 1)], u1, v1)
    v3 = over_grid(v2[2], FROM_AHEAD)
    *u2, acc = lax.optimization_barrier((*u2, acc))
    u3 = over_grid(u2[2], FROM_AHEAD)
    acc = add(acc, [chip(2, 0), chip(-side, 1), chip(side, 1)], u2, v2)
    own, sib, q = call(
        column_kernel,
        [sds((ROWS, 2 * HC), F32)] * 2 + [sds((16, 32, BIG + HB), F32)],
        [
            (structure, "s"),
            (widths, "s"),
            (acc, "v"),
            (a_own, (0,)),
            (a_sib, (0,)),
            (u3, "v"),
            (v3, "v"),
            (big, "v"),
            (small, "v"),
        ],
        "column",
        flops=2 * 4 * ROWS * 2 * ROWS * 2 * HC + 2 * 2 * 1024 * 2 * ROWS * 768,
        scratch=[
            pltpu.VMEM((2 * ROWS, 2 * HC), BF16),
            pltpu.VMEM((2, 2 * ROWS, 2 * HC), BF16),
            pltpu.VMEM((ROWS, 2 * HC), F32),
            pltpu.VMEM((ROWS, 2 * HC), F32),
            pltpu.VMEM((16, 32, BIG + HB), F32),
            pltpu.SemaphoreType.DMA((3,)),
        ],
        blocks=[chip(2, 1)],
        limit=20,
        out_space=pltpu.HBM,
    )
    other = over_grid(sib, CORE)
    sums = lax.all_to_all(q, "grid", 0, 0, tiled=True)
    column_inverse, d_keep, d_send = call(
        spread_kernel,
        [sds((2, ROWS, 3 * BIG), BF16)] + [sds((8, 48, 384), F32)] * 2,
        [(widths, "s"), (pole_weights, "s"), (own, "v"), (other, "v")],
        "spread",
        scratch=[pltpu.VMEM((ROWS, 3 * BIG), F32)],
    )
    d_got = lax.ppermute(d_send, "pole", Z_PAIR)
    sums, d_keep = lax.optimization_barrier((sums, d_keep))
    pivot_block, pay = call(
        pivot_kernel,
        [sds((2, 3, 32, BIG), F32), sds((8, 64, 384), F32)],
        [
            (widths, "s"),
            (pole_weights, "s"),
            (pivot_inverse[0], "v"),
            (sums, "v"),
            (d_keep, "v"),
            (d_got, "v"),
        ],
        "pivot",
        scratch=[pltpu.VMEM((96, BIG), F32)],
    )
    pays = lax.all_to_all(pay, "pole", 0, 0, axis_index_groups=Z_GROUPS, tiled=True)
    density_column, p_keep, p_send = call(
        density_kernel,
        [sds((ROWS, 96), F32)] + [sds((8, 384), F32)] * 2,
        [(pays, "v")],
        "density",
    )
    p_got = lax.ppermute(p_send, "pole", Z_PAIR)
    density_pivot = call(
        last_kernel, [sds((3, 32, 32), F32)], [(p_keep, "v"), (p_got, "v")], "last"
    )[0]
    return (column_inverse[None], pivot_block[None], density_column, density_pivot)


def solution(mesh):
    in_specs = (
        P("pole", None, "grid", None),
        P("pole", None, "grid", None),
        P("pole", None, None, "grid", None),
        P(),
        P(),
        P("pole", None),
    )
    out_specs = (
        P("pole", None, "grid", None),
        P("pole", None, None, "grid", None),
        P("grid", "pole"),
        P(None, "grid", "pole"),
    )
    return jax.shard_map(local, mesh=mesh, in_specs=in_specs, out_specs=out_specs, check_vma=False)
```

```python
import functools

import jax
import jax.numpy as jnp
from jax import lax
from jax.experimental import pallas as pl
from jax.experimental.pallas import tpu as pltpu
from jax.sharding import PartitionSpec as P

F32 = jnp.float32
BF16 = jnp.bfloat16
BIG = 512
ROWS = 192
HB = 256
HS = 128
HC = HB + HS

NX, NY, NCORE = 4, 2, 2
NZ, NH = 8, 2


def grid_perm(source):
    def at(y, x, c):
        return (y * NX + x % NX) * NCORE + c

    return [
        (at(*source(y, x, c)), at(y, x, c)) for y in range(NY) for x in range(NX) for c in range(NCORE)
    ]


CORE = grid_perm(lambda y, x, c: (y, x, 1 - c))
FROM_AHEAD = grid_perm(lambda y, x, c: (y, x + 1 - 2 * c, c))
FROM_BEHIND = grid_perm(lambda y, x, c: (y, x - 1 + 2 * c, c))
FROM_Y = grid_perm(lambda y, x, c: (1 - y, x, c))


def pole_perm(source):
    def at(z, h):
        return z * NH + h

    return [(at(*source(z, h)), at(z, h)) for z in range(NZ) for h in range(NH)]


def z_pair(bit):
    return pole_perm(lambda z, h: (z ^ bit, h))


def place():
    g = lax.axis_index("grid")
    c = lax.rem(g, 2)
    x = lax.rem(lax.div(g, 2), NX)
    y = lax.div(g, 2 * NX)
    return g, c, x, y


def z_bits():
    z = lax.div(lax.axis_index("pole"), NH)
    return lax.rem(z, 2), lax.rem(lax.div(z, 2), 2)


def supers(widths):
    kb = jnp.where(widths[0] == BIG, 0, jnp.where(widths[1] == BIG, 1, 2))
    k1 = jnp.where(kb == 0, 1, 0)
    k2 = jnp.where(kb == 2, 1, 2)
    return kb, k1, k2, widths[k1]


def iota(shape, axis):
    return lax.broadcasted_iota(jnp.int32, shape, axis)


def row_mask(structure, block, count, k, lanes):
    return jnp.concatenate(
        [jnp.full((32, lanes), structure[k, block + i].astype(F32), F32) for i in range(count)], axis=0
    )


def call(body, outs, ins, name, flops=0, scratch=(), limit=16, out_space=pltpu.VMEM):
    spaces = {"s": pltpu.SMEM, "v": pltpu.VMEM, "h": pltpu.HBM}
    size = sum(a.size * a.dtype.itemsize for a, _ in ins) + sum(
        o.size * o.dtype.itemsize for o in outs
    )
    if out_space is pltpu.HBM:
        outs = [pltpu.HBM(o.shape, o.dtype) for o in outs]
    return pl.pallas_call(
        body,
        out_shape=tuple(outs),
        in_specs=[pl.BlockSpec(memory_space=spaces[kind]) for _, kind in ins],
        out_specs=tuple(pl.BlockSpec(memory_space=out_space) for _ in outs),
        scratch_shapes=list(scratch),
        compiler_params=pltpu.CompilerParams(vmem_limit_bytes=limit * 1024 * 1024),
        cost_estimate=pl.CostEstimate(flops=flops, bytes_accessed=size, transcendentals=0),
        name=name,
    )(*[a for a, _ in ins])


def sds(shape, dtype):
    return jax.ShapeDtypeStruct(shape, dtype)


def prep_kernel(structure, widths, f, keep, send):
    g, c, _, _ = place()
    kb, k1, k2, a = supers(widths)
    base = g * 6
    mask_b = row_mask(structure, base, 6, kb, HB).astype(BF16)
    mask_1 = row_mask(structure, base, 6, k1, HB).astype(BF16)
    mask_2 = row_mask(structure, base, 6, k2, HB).astype(BF16)
    shift = (iota((HB, HB), 0) + a == iota((HB, HB), 1)).astype(BF16)
    first = iota((ROWS, HB), 1) < a

    def at(k, part):
        return pl.ds(pl.multiple_of(k * BIG + part * HB, HB), HB)

    for p in range(2):
        o = p * HC
        keep[:, o : o + HB] = f[p, :, at(kb, c)] * mask_b
        send[:, o : o + HB] = f[p, :, at(kb, 1 - c)] * mask_b
        one = (f[p, :, at(k1, 0)] * mask_1).astype(F32)
        two = jnp.dot(f[p, :, at(k2, 0)] * mask_2, shift, preferred_element_type=F32)
        small = jnp.where(first, one, two)
        low, high = small[:, :HS], small[:, HS:]
        keep[:, o + HB : o + HC] = jnp.where(c == 0, low, high).astype(BF16)
        send[:, o + HB : o + HC] = jnp.where(c == 0, high, low).astype(BF16)


def left_kernel(widths, keep, send, got_mine, got_theirs, big, small):
    _, c, _, _ = place()
    _, _, _, a = supers(widths)
    back = (iota((HB, HB), 0) == iota((HB, HB), 1) + a).astype(BF16)
    mine = jnp.concatenate([keep[...], got_mine[...]], axis=0)
    theirs = jnp.concatenate([send[...], got_theirs[...]], axis=0)
    for p in range(2):
        o = p * HC
        for part, half in ((c, mine), (1 - c, theirs)):
            at = pl.ds(pl.multiple_of((2 * part + p) * HB, HB), HB)
            big[at, :] = half[:, o : o + HB].astype(F32).T.astype(BF16)
        m, t = mine[:, o + HB : o + HC].astype(F32), theirs[:, o + HB : o + HC].astype(F32)
        low, high = jnp.where(c == 0, m, t), jnp.where(c == 0, t, m)
        both = jnp.concatenate([low, high], axis=1)
        moved = jnp.dot(both.astype(BF16), back, preferred_element_type=F32)
        small[p * HB : (p + 1) * HB] = both.T.astype(BF16)
        small[(2 + p) * HB : (3 + p) * HB] = moved.T.astype(BF16)


def rows_at(bit, count):
    return pl.ds(pl.multiple_of(bit * count, count), count)


def block_copies(offsets, a_own, a_sib, us, vs, left, rows, sems):
    _, c, x, y = place()
    side = 1 - 2 * c
    copies = []
    for i, (dx, dy) in enumerate(offsets):
        at = lax.rem(y + dy, NY) * NX + lax.rem(x + dx * side + NX, NX)
        cols = pl.ds(pl.multiple_of(at * 2 * ROWS, 2 * ROWS), 2 * ROWS)
        pairs = [
            (us[i], rows.at[i, rows_at(c, ROWS)]),
            (vs[i], rows.at[i, rows_at(1 - c, ROWS)]),
            (a_own.at[:, cols], left.at[i, : 2 * ROWS]),
            (a_sib.at[:, cols], left.at[i, 2 * ROWS :]),
        ]
        copies += [pltpu.make_async_copy(v, to, sems.at[4 * i + j]) for j, (v, to) in enumerate(pairs)]
    return copies


def add_blocks(copies, left, rows, get, put):
    z = None
    for i in range(len(copies) // 4):
        for copy in copies[4 * i : 4 * i + 4]:
            copy.wait()
        d = jnp.dot(left[i], rows[i], preferred_element_type=F32)
        z = d if z is None else z + d
    for s in range(2):
        re, im = z[2 * s * ROWS : (2 * s + 1) * ROWS], z[(2 * s + 1) * ROWS : (2 * s + 2) * ROWS]
        old_re, old_im = get(s)
        put(s, old_re + (re[:, :HC] - im[:, HC:]), old_im + (re[:, HC:] + im[:, :HC]))


def acc_kernel(offsets, has_acc, *refs):
    refs = list(refs)
    old = refs.pop(0) if has_acc else None
    n = len(offsets)
    a_own, a_sib, us, vs = refs[0], refs[1], refs[2 : 2 + n], refs[2 + n : 2 + 2 * n]
    out, left, rows, sems = refs[2 + 2 * n :]
    copies = block_copies(offsets, a_own, a_sib, us, vs, left, rows, sems)
    for copy in copies:
        copy.start()

    def get(s):
        if old is None:
            return 0.0, 0.0
        return old[s, :, :HC], old[s, :, HC:]

    def put(s, re, im):
        out[s, :, :HC] = re
        out[s, :, HC:] = im

    add_blocks(copies, left, rows, get, put)


def column_kernel(structure, widths, old, a_own, a_sib, u, v, big_in, small_in, own_out, sib_out, q_out, *scratch):
    left, rows, big, small, gs, own, sib, q, sems, in_sems = scratch
    g, c, _, _ = place()
    kb, k1, k2, a = supers(widths)

    def get(s):
        return old[s, :, :HC], old[s, :, HC:]

    def put(s, re, im):
        base = (g + s * (1 - 2 * c)) * 6
        mask_b = row_mask(structure, base, 6, kb, HB)
        mask_1 = row_mask(structure, base, 6, k1, HS)
        mask_2 = row_mask(structure, base, 6, k2, HS)
        mask_s = jnp.where(iota((ROWS, HS), 1) + c * HS < a, mask_1, mask_2)
        out = own if s == 0 else sib
        for p, w in ((0, re), (1, im)):
            vb = -(w[:, :HB] * mask_b)
            vs = -(w[:, HB:] * mask_s)
            out[:, p * HC : p * HC + HB] = vb
            out[:, p * HC + HB : (p + 1) * HC] = vs
            for part, lo, hi in ((vb, p * HB, (p + 1) * HB), (vs, 2 * HB + p * HS, 2 * HB + (p + 1) * HS)):
                top = part.astype(BF16)
                gs[s * ROWS : (s + 1) * ROWS, lo:hi] = top
                gs[(s + 2) * ROWS : (s + 3) * ROWS, lo:hi] = (part - top.astype(F32)).astype(BF16)

    blocks = block_copies([(2, 1)], a_own, a_sib, [u], [v], left, rows, in_sems)
    lefts = [
        pltpu.make_async_copy(big_in, big, in_sems.at[4]),
        pltpu.make_async_copy(small_in, small, in_sems.at[5]),
    ]
    for copy in blocks + lefts:
        copy.start()
    add_blocks(blocks, left, rows, get, put)
    copies = [pltpu.make_async_copy(sib, sib_out, sems.at[0]), pltpu.make_async_copy(own, own_out, sems.at[1])]
    for copy in copies:
        copy.start()

    def across(left, lo, hi):
        twice = jnp.concatenate([left[...], left[...]], axis=1)
        return jnp.dot(twice, gs[:, lo:hi], preferred_element_type=F32)

    lefts[0].wait()
    z = across(big, 0, BIG)
    for h in range(2):
        re, im = z[2 * h * HB : (2 * h + 1) * HB], z[(2 * h + 1) * HB : (2 * h + 2) * HB]
        for t in range(8):
            r = slice(32 * t, 32 * t + 32)
            q[8 * h + t, :, :HB] = re[r, :HB] - im[r, HB:]
            q[8 * h + t, :, HB:BIG] = re[r, HB:] + im[r, :HB]
    copies.append(pltpu.make_async_copy(q.at[:, :, :BIG], q_out.at[:, :, :BIG], sems.at[2]))
    copies[2].start()
    lefts[1].wait()
    z = across(small, BIG, BIG + HB)
    col = iota((HB, HS), 1) + c * HS
    row = iota((HB, HS), 0)
    parts = []
    for i in range(2):
        re, im = z[2 * i * HB : (2 * i + 1) * HB], z[(2 * i + 1) * HB : (2 * i + 2) * HB]
        parts.append((re[:, :HS] - im[:, HS:], re[:, HS:] + im[:, :HS]))
    for p in range(2):
        e = jnp.where(
            col < a, jnp.where(row < a, parts[0][p], 0.0), jnp.where(row < HB - a, parts[1][p], 0.0)
        )
        at = slice(BIG + p * HS, BIG + (p + 1) * HS)
        for t in range(8):
            q[t, :, at] = e[32 * t : 32 * t + 32]
            q[8 + t, :, at] = jnp.zeros((32, HS), F32)
    copies.append(pltpu.make_async_copy(q.at[:, :, BIG:], q_out.at[:, :, BIG:], sems.at[3]))
    copies[3].start()
    for copy in copies:
        copy.wait()


def spread_kernel(widths, weights, mine, other, out, keep, send, wide):
    _, c, _, _ = place()
    odd, _ = z_bits()
    kb, k1, k2, a = supers(widths)
    wr, wi = weights[0, 0], weights[0, 1]
    back = (iota((HB, HB), 0) == iota((HB, HB), 1) + a).astype(BF16)
    lane = iota((ROWS, HB), 1)
    halves = []
    for ref in (mine, other):
        halves.append([(ref[:, p * HC : p * HC + HB], ref[:, p * HC + HB : (p + 1) * HC]) for p in range(2)])

    def at(k, part):
        return pl.ds(pl.multiple_of(k * BIG + part * HB, HB), HB)

    zero = jnp.zeros((ROWS, HB), BF16)
    small = []
    for p in range(2):
        m, t = halves[0][p], halves[1][p]
        out[p, :, at(kb, c)] = m[0].astype(BF16)
        out[p, :, at(kb, 1 - c)] = t[0].astype(BF16)
        low, high = jnp.where(c == 0, m[1], t[1]), jnp.where(c == 0, t[1], m[1])
        s = jnp.concatenate([low, high], axis=1)
        sb = s.astype(BF16)
        out[p, :, at(k1, 0)] = jnp.where(lane < a, s, 0.0).astype(BF16)
        out[p, :, at(k1, 1)] = zero
        out[p, :, at(k2, 0)] = jnp.dot(sb, back, preferred_element_type=F32).astype(BF16)
        out[p, :, at(k2, 1)] = zero
        small.append(s)
    for i, part in ((0, c), (1, 1 - c)):
        wide[:, at(0, part)] = wr * halves[i][1][0] + wi * halves[i][0][0]
    wide[:, BIG:] = wr * small[1] + wi * small[0]
    keep[...] = wide[rows_at(odd, 96), :]
    send[...] = wide[rows_at(1 - odd, 96), :]


def second_kernel(old, got, keep, send, total):
    _, bit = z_bits()
    total[...] = old[...] + got[...]
    keep[...] = total[rows_at(bit, 48), :]
    send[...] = total[rows_at(1 - bit, 48), :]


def pivot_kernel(widths, weights, pivot, sums, keep, got, block, pay, wide, column):
    g = lax.axis_index("grid")
    kb, k1, k2, a = supers(widths)
    wr, wi = weights[0, 0], weights[0, 1]
    m, t = sums[0], sums[1]
    for i in range(1, 8):
        m, t = m + sums[2 * i], t + sums[2 * i + 1]
    row = iota((32, BIG), 0) + g * 32
    line = iota((32, BIG), 1)
    blank = jnp.zeros((32, HB), F32)
    q = []
    for p in range(2):
        full = jnp.concatenate([u[:, p * HB : (p + 1) * HB] for u in (m, t)], axis=1)
        e = jnp.concatenate([u[:, BIG + p * HS : BIG + (p + 1) * HS] for u in (m, t)], axis=1)
        moved = pltpu.roll(e, HB - a, 1)
        q.append((full, jnp.concatenate([e, blank], axis=1), jnp.concatenate([moved, blank], axis=1)))
    for i, (k, w) in enumerate(((kb, BIG), (k1, a), (k2, HB - a))):
        live = (row < w) & (line < w)
        blocks = []
        for p in range(2):
            b = jnp.where(live, pivot[p, k] - q[p][i], 0.0)
            block[p, k] = b
            blocks.append(b)
        wide[pl.ds(pl.multiple_of(k * 32, 32), 32), :] = wr * blocks[1] + wi * blocks[0]
    d = keep[...] + got[...]
    lane = iota((48, HB), 1)
    small = d[:, BIG:]
    none = jnp.zeros((48, HB), F32)

    def at(k, part):
        return pl.ds(pl.multiple_of(k * BIG + part * HB, HB), HB)

    for part in range(2):
        column[:, at(kb, part)] = d[:, part * HB : (part + 1) * HB]
    column[:, at(k1, 0)] = jnp.where(lane < a, small, 0.0)
    column[:, at(k1, 1)] = none
    column[:, at(k2, 0)] = jnp.where(lane < HB - a, pltpu.roll(small, HB - a, 1), 0.0)
    column[:, at(k2, 1)] = none
    v, w = column[...], wide[...]
    pad = jnp.zeros((16, 32), F32)
    for p in range(16):
        parts = [v[16 * i : 16 * i + 16, 96 * p : 96 * p + 96] for i in range(3)]
        parts += [w[16 * i : 16 * i + 16, 32 * p : 32 * p + 32] for i in range(6)]
        pay[p] = jnp.concatenate(parts + [pad], axis=1)


def density_kernel(pays, column, pivot):
    total = pays[0]
    for p in range(1, 16):
        total = total + pays[p]
    for b0 in range(2):
        for b1 in range(2):
            part = [pays[(b0 + 2 * b1 + 4 * b2) * NH + h] for b2 in range(2) for h in range(NH)]
            v = (part[0] + part[1]) + (part[2] + part[3])
            for i in range(3):
                row = 96 * b0 + 48 * b1 + 16 * i
                column[row : row + 16] = v[:, 96 * i : 96 * i + 96]
    for i in range(6):
        pivot[i // 2, 16 * (i % 2) : 16 * (i % 2) + 16] = total[:, 288 + 32 * i : 320 + 32 * i]


def local(factor_cols, ancestor_inverse, pivot_inverse, structure, widths, pole_weights):
    structure = structure.T

    def over_grid(v, perm):
        return lax.ppermute(v, "grid", perm)

    block = sds((ROWS, 2 * HC), BF16)
    keep, send = call(
        prep_kernel,
        [block, block],
        [(structure, "s"), (widths, "s"), (factor_cols[0], "v")],
        "prep",
        flops=2 * 2 * ROWS * HB * HB,
    )
    a_own = ancestor_inverse[0].reshape(2 * ROWS, -1)
    a_sib = over_grid(a_own, CORE)
    keep, send, a_sib = lax.optimization_barrier((keep, send, a_sib))
    got_mine, got_theirs = over_grid(send, CORE), over_grid(keep, CORE)
    got_mine, got_theirs = lax.optimization_barrier((got_mine, got_theirs))

    def first(v):
        return [over_grid(v, perm) for perm in (FROM_AHEAD, FROM_BEHIND, FROM_Y)]

    def second(ahead, behind, beside):
        return [over_grid(ahead, FROM_AHEAD), over_grid(beside, FROM_BEHIND), over_grid(ahead, FROM_Y)]

    def add(old, offsets, us, vs):
        n = len(offsets)
        ins = ([] if old is None else [(old, "v")]) + [(a, "h") for a in (a_own, a_sib)]
        ins += [(b, "h") for b in (*us, *vs)]
        return call(
            functools.partial(acc_kernel, offsets, old is not None),
            [sds((2, ROWS, 2 * HC), F32)],
            ins,
            "product",
            flops=2 * n * 4 * ROWS * 2 * ROWS * 2 * HC,
            scratch=[
                pltpu.VMEM((n, 4 * ROWS, 2 * ROWS), BF16),
                pltpu.VMEM((n, 2 * ROWS, 2 * HC), BF16),
                pltpu.SemaphoreType.DMA((4 * n,)),
            ],
        )[0]

    v1 = first(got_mine)
    u1 = first(keep)
    v2 = second(*v1)
    acc = add(None, [(0, 0)], [keep], [got_mine])
    big, small = call(
        left_kernel,
        [sds((4 * HB, 2 * ROWS), BF16)] * 2,
        [(widths, "s"), (keep, "v"), (send, "v"), (got_mine, "v"), (got_theirs, "v")],
        "left",
        flops=2 * 2 * 2 * ROWS * HB * HB,
    )
    *u1, acc, big, small = lax.optimization_barrier((*u1, acc, big, small))
    u2 = second(*u1)
    acc = add(acc, [(1, 0), (-1, 0), (0, 1)], u1, v1)
    v3 = over_grid(v2[2], FROM_AHEAD)
    *u2, acc = lax.optimization_barrier((*u2, acc))
    u3 = over_grid(u2[2], FROM_AHEAD)
    acc = add(acc, [(2, 0), (-1, 1), (1, 1)], u2, v2)
    own, sib, q = call(
        column_kernel,
        [sds((ROWS, 2 * HC), F32)] * 2 + [sds((16, 32, BIG + HB), F32)],
        [
            (structure, "s"),
            (widths, "s"),
            (acc, "v"),
            (a_own, "h"),
            (a_sib, "h"),
            (u3, "h"),
            (v3, "h"),
            (big, "h"),
            (small, "h"),
        ],
        "column",
        flops=2 * 4 * ROWS * 2 * ROWS * 2 * HC + 2 * 2 * 1024 * 2 * ROWS * 768,
        scratch=[
            pltpu.VMEM((1, 4 * ROWS, 2 * ROWS), BF16),
            pltpu.VMEM((1, 2 * ROWS, 2 * HC), BF16),
            pltpu.VMEM((4 * HB, 2 * ROWS), BF16),
            pltpu.VMEM((4 * HB, 2 * ROWS), BF16),
            pltpu.VMEM((4 * ROWS, 2 * HC), BF16),
            pltpu.VMEM((ROWS, 2 * HC), F32),
            pltpu.VMEM((ROWS, 2 * HC), F32),
            pltpu.VMEM((16, 32, BIG + HB), F32),
            pltpu.SemaphoreType.DMA((4,)),
            pltpu.SemaphoreType.DMA((6,)),
        ],
        limit=20,
        out_space=pltpu.HBM,
    )
    other = over_grid(sib, CORE)
    sums = lax.all_to_all(q, "grid", 0, 0, tiled=True)
    column_inverse, d_keep, d_send = call(
        spread_kernel,
        [sds((2, ROWS, 3 * BIG), BF16)] + [sds((96, 768), F32)] * 2,
        [(widths, "s"), (pole_weights, "s"), (own, "v"), (other, "v")],
        "spread",
        scratch=[pltpu.VMEM((ROWS, 768), F32)],
    )
    d_got = lax.ppermute(d_send, "pole", z_pair(1))
    d_keep, d_send = call(
        second_kernel,
        [sds((48, 768), F32)] * 2,
        [(d_keep, "v"), (d_got, "v")],
        "second",
        scratch=[pltpu.VMEM((96, 768), F32)],
    )
    d_got = lax.ppermute(d_send, "pole", z_pair(2))
    sums, d_keep = lax.optimization_barrier((sums, d_keep))
    pivot_block, pay = call(
        pivot_kernel,
        [sds((2, 3, 32, BIG), F32), sds((16, 16, 512), F32)],
        [
            (widths, "s"),
            (pole_weights, "s"),
            (pivot_inverse[0], "v"),
            (sums, "v"),
            (d_keep, "v"),
            (d_got, "v"),
        ],
        "pivot",
        scratch=[pltpu.VMEM((96, BIG), F32), pltpu.VMEM((48, 3 * BIG), F32)],
    )
    pays = lax.all_to_all(pay, "pole", 0, 0, tiled=True)
    density_column, density_pivot = call(
        density_kernel, [sds((ROWS, 96), F32), sds((3, 32, 32), F32)], [(pays, "v")], "density"
    )
    return (column_inverse[None], pivot_block[None], density_column, density_pivot)


def solution(mesh):
    in_specs = (
        P("pole", None, "grid", None),
        P("pole", None, "grid", None),
        P("pole", None, None, "grid", None),
        P(),
        P(),
        P("pole", None),
    )
    out_specs = (
        P("pole", None, "grid", None),
        P("pole", None, None, "grid", None),
        P("grid", "pole"),
        P(None, "grid", "pole"),
    )
    return jax.shard_map(local, mesh=mesh, in_specs=in_specs, out_specs=out_specs, check_vma=False)
```

```python
import functools

import jax
import jax.numpy as jnp
from jax import lax
from jax.experimental import pallas as pl
from jax.experimental.pallas import tpu as pltpu
from jax.sharding import PartitionSpec as P

F32 = jnp.float32
BF16 = jnp.bfloat16
BIG = 512
ROWS = 192
HB = 256
HS = 128
HC = HB + HS

NX, NY, NCORE = 4, 2, 2
NZ, NH = 8, 2


def grid_perm(source):
    def at(y, x, c):
        return (y * NX + x % NX) * NCORE + c

    return [
        (at(*source(y, x, c)), at(y, x, c)) for y in range(NY) for x in range(NX) for c in range(NCORE)
    ]


CORE = grid_perm(lambda y, x, c: (y, x, 1 - c))
FROM_AHEAD = grid_perm(lambda y, x, c: (y, x + 1 - 2 * c, c))
FROM_BEHIND = grid_perm(lambda y, x, c: (y, x - 1 + 2 * c, c))
FROM_FAR = grid_perm(lambda y, x, c: (y, x + 2, c))
FROM_Y = grid_perm(lambda y, x, c: (1 - y, x, c))


def pole_perm(source):
    def at(z, h):
        return z * NH + h

    return [(at(*source(z, h)), at(z, h)) for z in range(NZ) for h in range(NH)]


def z_pair(bit):
    return pole_perm(lambda z, h: (z ^ bit, h))


def place():
    g = lax.axis_index("grid")
    c = lax.rem(g, 2)
    x = lax.rem(lax.div(g, 2), NX)
    y = lax.div(g, 2 * NX)
    return g, c, x, y


def z_bits():
    z = lax.div(lax.axis_index("pole"), NH)
    return lax.rem(z, 2), lax.rem(lax.div(z, 2), 2)


def supers(widths):
    kb = jnp.where(widths[0] == BIG, 0, jnp.where(widths[1] == BIG, 1, 2))
    k1 = jnp.where(kb == 0, 1, 0)
    k2 = jnp.where(kb == 2, 1, 2)
    return kb, k1, k2, widths[k1]


def iota(shape, axis):
    return lax.broadcasted_iota(jnp.int32, shape, axis)


def row_mask(structure, block, count, k, lanes):
    return jnp.concatenate(
        [jnp.full((32, lanes), structure[k, block + i].astype(F32), F32) for i in range(count)], axis=0
    )


def call(body, outs, ins, name, flops=0, scratch=(), limit=16, out_space=pltpu.VMEM):
    spaces = {"s": pltpu.SMEM, "v": pltpu.VMEM, "h": pltpu.HBM, "p": pltpu.HBM}
    size = sum(a.size * a.dtype.itemsize for a, _ in ins) + sum(
        o.size * o.dtype.itemsize for o in outs
    )
    if out_space is pltpu.HBM:
        outs = [pltpu.HBM(o.shape, o.dtype) for o in outs]
    return pl.pallas_call(
        body,
        out_shape=tuple(outs),
        in_specs=[pl.BlockSpec(memory_space=spaces[kind]) for _, kind in ins],
        out_specs=tuple(pl.BlockSpec(memory_space=out_space) for _ in outs),
        scratch_shapes=list(scratch),
        compiler_params=pltpu.CompilerParams(vmem_limit_bytes=limit * 1024 * 1024),
        cost_estimate=pl.CostEstimate(flops=flops, bytes_accessed=size, transcendentals=0),
        name=name,
    )(*[pltpu.with_memory_space_constraint(a, pltpu.HBM) if kind == "p" else a for a, kind in ins])


def sds(shape, dtype):
    return jax.ShapeDtypeStruct(shape, dtype)


def prep_kernel(structure_in, widths_in, f_in, keep, send, structure, widths, f, sems):
    pairs = ((widths_in, widths), (structure_in, structure), (f_in, f))
    copies = [pltpu.make_async_copy(v, to, sems.at[i]) for i, (v, to) in enumerate(pairs)]
    for copy in copies:
        copy.start()
    for copy in copies:
        copy.wait()
    g, c, _, _ = place()
    kb, k1, k2, a = supers(widths)
    base = g * 6
    mask_b = row_mask(structure, base, 6, kb, HB).astype(BF16)
    mask_1 = row_mask(structure, base, 6, k1, HB).astype(BF16)
    mask_2 = row_mask(structure, base, 6, k2, HB).astype(BF16)
    shift = (iota((HB, HB), 0) + a == iota((HB, HB), 1)).astype(BF16)
    first = iota((ROWS, HB), 1) < a

    def at(k, part):
        return pl.ds(pl.multiple_of(k * BIG + part * HB, HB), HB)

    for p in range(2):
        o = p * HC
        keep[:, o : o + HB] = f[p, :, at(kb, c)] * mask_b
        send[:, o : o + HB] = f[p, :, at(kb, 1 - c)] * mask_b
        one = (f[p, :, at(k1, 0)] * mask_1).astype(F32)
        two = jnp.dot(f[p, :, at(k2, 0)] * mask_2, shift, preferred_element_type=F32)
        small = jnp.where(first, one, two)
        low, high = small[:, :HS], small[:, HS:]
        keep[:, o + HB : o + HC] = jnp.where(c == 0, low, high).astype(BF16)
        send[:, o + HB : o + HC] = jnp.where(c == 0, high, low).astype(BF16)


def left_kernel(widths, keep, send, got_mine, got_theirs, big, small):
    _, c, _, _ = place()
    _, _, _, a = supers(widths)
    back = (iota((HB, HB), 0) == iota((HB, HB), 1) + a).astype(BF16)
    mine = jnp.concatenate([keep[...], got_mine[...]], axis=0)
    theirs = jnp.concatenate([send[...], got_theirs[...]], axis=0)
    for p in range(2):
        o = p * HC
        for part, half in ((c, mine), (1 - c, theirs)):
            at = pl.ds(pl.multiple_of((2 * part + p) * HB, HB), HB)
            big[at, :] = half[:, o : o + HB].astype(F32).T.astype(BF16)
        m, t = mine[:, o + HB : o + HC].astype(F32), theirs[:, o + HB : o + HC].astype(F32)
        low, high = jnp.where(c == 0, m, t), jnp.where(c == 0, t, m)
        both = jnp.concatenate([low, high], axis=1)
        moved = jnp.dot(both.astype(BF16), back, preferred_element_type=F32)
        small[p * HB : (p + 1) * HB] = both.T.astype(BF16)
        small[(2 + p) * HB : (3 + p) * HB] = moved.T.astype(BF16)


def rows_at(bit, count):
    return pl.ds(pl.multiple_of(bit * count, count), count)


def block_copies(offsets, a_own, a_sib, us, vs, left, rows, sems):
    _, c, x, y = place()
    side = 1 - 2 * c
    copies = []
    for i, (dx, dy) in enumerate(offsets):
        at = lax.rem(y + dy, NY) * NX + lax.rem(x + dx * side + NX, NX)
        cols = pl.ds(pl.multiple_of(at * 2 * ROWS, 2 * ROWS), 2 * ROWS)
        pairs = [
            (us[i], rows.at[i, rows_at(c, ROWS)]),
            (vs[i], rows.at[i, rows_at(1 - c, ROWS)]),
            (a_own.at[:, cols], left.at[i, : 2 * ROWS]),
            (a_sib.at[:, cols], left.at[i, 2 * ROWS :]),
        ]
        copies += [pltpu.make_async_copy(v, to, sems.at[4 * i + j]) for j, (v, to) in enumerate(pairs)]
    return copies


def add_blocks(copies, left, rows, get, put):
    z = None
    for i in range(len(copies) // 4):
        for copy in copies[4 * i : 4 * i + 4]:
            copy.wait()
        d = jnp.dot(left[i], rows[i], preferred_element_type=F32)
        z = d if z is None else z + d
    for s in range(2):
        re, im = z[2 * s * ROWS : (2 * s + 1) * ROWS], z[(2 * s + 1) * ROWS : (2 * s + 2) * ROWS]
        old_re, old_im = get(s)
        put(s, old_re + (re[:, :HC] - im[:, HC:]), old_im + (re[:, HC:] + im[:, :HC]))


def acc_kernel(offsets, has_acc, *refs):
    refs = list(refs)
    old = refs.pop(0) if has_acc else None
    n = len(offsets)
    a_own, a_sib, us, vs = refs[0], refs[1], refs[2 : 2 + n], refs[2 + n : 2 + 2 * n]
    out, left, rows, sems = refs[2 + 2 * n :]
    copies = block_copies(offsets, a_own, a_sib, us, vs, left, rows, sems)
    for copy in copies:
        copy.start()

    def get(s):
        if old is None:
            return 0.0, 0.0
        return old[s, :, :HC], old[s, :, HC:]

    def put(s, re, im):
        out[s, :, :HC] = re
        out[s, :, HC:] = im

    add_blocks(copies, left, rows, get, put)


def column_kernel(structure, widths, old, a_own, a_sib, u, v, big_in, small_in, own_out, sib_out, q_out, *scratch):
    left, rows, big, small, gs, own, sib, q, sems, in_sems = scratch
    g, c, _, _ = place()
    kb, k1, k2, a = supers(widths)

    def get(s):
        return old[s, :, :HC], old[s, :, HC:]

    def put(s, re, im):
        base = (g + s * (1 - 2 * c)) * 6
        mask_b = row_mask(structure, base, 6, kb, HB)
        mask_1 = row_mask(structure, base, 6, k1, HS)
        mask_2 = row_mask(structure, base, 6, k2, HS)
        mask_s = jnp.where(iota((ROWS, HS), 1) + c * HS < a, mask_1, mask_2)
        out = own if s == 0 else sib
        for p, w in ((0, re), (1, im)):
            vb = -(w[:, :HB] * mask_b)
            vs = -(w[:, HB:] * mask_s)
            out[:, p * HC : p * HC + HB] = vb
            out[:, p * HC + HB : (p + 1) * HC] = vs
            for part, lo, hi in ((vb, p * HB, (p + 1) * HB), (vs, 2 * HB + p * HS, 2 * HB + (p + 1) * HS)):
                top = part.astype(BF16)
                gs[s * ROWS : (s + 1) * ROWS, lo:hi] = top
                gs[(s + 2) * ROWS : (s + 3) * ROWS, lo:hi] = (part - top.astype(F32)).astype(BF16)

    blocks = block_copies([(2, 1)], a_own, a_sib, [u], [v], left, rows, in_sems)
    lefts = [
        pltpu.make_async_copy(big_in, big, in_sems.at[4]),
        pltpu.make_async_copy(small_in, small, in_sems.at[5]),
    ]
    for copy in blocks + lefts:
        copy.start()
    add_blocks(blocks, left, rows, get, put)
    copies = [pltpu.make_async_copy(sib, sib_out, sems.at[0]), pltpu.make_async_copy(own, own_out, sems.at[1])]
    for copy in copies:
        copy.start()

    def across(left, lo, hi):
        twice = jnp.concatenate([left[...], left[...]], axis=1)
        return jnp.dot(twice, gs[:, lo:hi], preferred_element_type=F32)

    lefts[0].wait()
    z = across(big, 0, BIG)
    for h in range(2):
        re, im = z[2 * h * HB : (2 * h + 1) * HB], z[(2 * h + 1) * HB : (2 * h + 2) * HB]
        for t in range(8):
            r = slice(32 * t, 32 * t + 32)
            q[8 * h + t, :, :HB] = re[r, :HB] - im[r, HB:]
            q[8 * h + t, :, HB:BIG] = re[r, HB:] + im[r, :HB]
    copies.append(pltpu.make_async_copy(q.at[:, :, :BIG], q_out.at[:, :, :BIG], sems.at[2]))
    copies[2].start()
    lefts[1].wait()
    z = across(small, BIG, BIG + HB)
    col = iota((HB, HS), 1) + c * HS
    row = iota((HB, HS), 0)
    parts = []
    for i in range(2):
        re, im = z[2 * i * HB : (2 * i + 1) * HB], z[(2 * i + 1) * HB : (2 * i + 2) * HB]
        parts.append((re[:, :HS] - im[:, HS:], re[:, HS:] + im[:, :HS]))
    for p in range(2):
        e = jnp.where(
            col < a, jnp.where(row < a, parts[0][p], 0.0), jnp.where(row < HB - a, parts[1][p], 0.0)
        )
        at = slice(BIG + p * HS, BIG + (p + 1) * HS)
        for t in range(8):
            q[t, :, at] = e[32 * t : 32 * t + 32]
            q[8 + t, :, at] = jnp.zeros((32, HS), F32)
    copies.append(pltpu.make_async_copy(q.at[:, :, BIG:], q_out.at[:, :, BIG:], sems.at[3]))
    copies[3].start()
    for copy in copies:
        copy.wait()


def halves_of(mine, other):
    return [
        [(ref[:, p * HC : p * HC + HB], ref[:, p * HC + HB : (p + 1) * HC]) for p in range(2)]
        for ref in (mine, other)
    ]


def in_order(c, first, second):
    return jnp.concatenate([jnp.where(c == 0, first, second), jnp.where(c == 0, second, first)], axis=1)


def term_kernel(weights, mine, other, keep, send, wide):
    _, c, _, _ = place()
    odd, _ = z_bits()
    wr, wi = weights[0, 0], weights[0, 1]
    m, t = ([wr * half[1][i] + wi * half[0][i] for i in range(2)] for half in halves_of(mine, other))
    wide[:, :BIG] = in_order(c, m[0], t[0])
    wide[:, BIG:] = in_order(c, m[1], t[1])
    keep[...] = wide[rows_at(odd, 96), :]
    send[...] = wide[rows_at(1 - odd, 96), :]


def spread_kernel(widths, mine, other, out):
    _, c, _, _ = place()
    kb, k1, k2, a = supers(widths)
    back = (iota((HB, HB), 0) == iota((HB, HB), 1) + a).astype(BF16)
    lane = iota((ROWS, HB), 1)

    def at(k, part):
        return pl.ds(pl.multiple_of(k * BIG + part * HB, HB), HB)

    zero = jnp.zeros((ROWS, HB), BF16)
    halves = halves_of(mine, other)
    for p in range(2):
        m, t = halves[0][p], halves[1][p]
        out[p, :, at(kb, c)] = m[0].astype(BF16)
        out[p, :, at(kb, 1 - c)] = t[0].astype(BF16)
        s = in_order(c, m[1], t[1])
        out[p, :, at(k1, 0)] = jnp.where(lane < a, s, 0.0).astype(BF16)
        out[p, :, at(k1, 1)] = zero
        out[p, :, at(k2, 0)] = jnp.dot(s.astype(BF16), back, preferred_element_type=F32).astype(BF16)
        out[p, :, at(k2, 1)] = zero


def second_kernel(old, got, keep, send, total):
    _, bit = z_bits()
    total[...] = old[...] + got[...]
    keep[...] = total[rows_at(bit, 48), :]
    send[...] = total[rows_at(1 - bit, 48), :]


def pivot_kernel(widths, weights, pivot, sums, keep, got, block, pay, wide, column):
    g = lax.axis_index("grid")
    kb, k1, k2, a = supers(widths)
    wr, wi = weights[0, 0], weights[0, 1]
    m, t = sums[0], sums[1]
    for i in range(1, 8):
        m, t = m + sums[2 * i], t + sums[2 * i + 1]
    row = iota((32, BIG), 0) + g * 32
    line = iota((32, BIG), 1)
    blank = jnp.zeros((32, HB), F32)
    q = []
    for p in range(2):
        full = jnp.concatenate([u[:, p * HB : (p + 1) * HB] for u in (m, t)], axis=1)
        e = jnp.concatenate([u[:, BIG + p * HS : BIG + (p + 1) * HS] for u in (m, t)], axis=1)
        moved = pltpu.roll(e, HB - a, 1)
        q.append((full, jnp.concatenate([e, blank], axis=1), jnp.concatenate([moved, blank], axis=1)))
    for i, (k, w) in enumerate(((kb, BIG), (k1, a), (k2, HB - a))):
        live = (row < w) & (line < w)
        blocks = []
        for p in range(2):
            b = jnp.where(live, pivot[p, k] - q[p][i], 0.0)
            block[p, k] = b
            blocks.append(b)
        wide[pl.ds(pl.multiple_of(k * 32, 32), 32), :] = wr * blocks[1] + wi * blocks[0]
    d = keep[...] + got[...]
    lane = iota((48, HB), 1)
    small = d[:, BIG:]
    none = jnp.zeros((48, HB), F32)

    def at(k, part):
        return pl.ds(pl.multiple_of(k * BIG + part * HB, HB), HB)

    for part in range(2):
        column[:, at(kb, part)] = d[:, part * HB : (part + 1) * HB]
    column[:, at(k1, 0)] = jnp.where(lane < a, small, 0.0)
    column[:, at(k1, 1)] = none
    column[:, at(k2, 0)] = jnp.where(lane < HB - a, pltpu.roll(small, HB - a, 1), 0.0)
    column[:, at(k2, 1)] = none
    v, w = column[...], wide[...]
    pad = jnp.zeros((16, 32), F32)
    for p in range(16):
        parts = [v[16 * i : 16 * i + 16, 96 * p : 96 * p + 96] for i in range(3)]
        parts += [w[16 * i : 16 * i + 16, 32 * p : 32 * p + 32] for i in range(6)]
        pay[p] = jnp.concatenate(parts + [pad], axis=1)


def density_kernel(pays, column, pivot):
    total = pays[0]
    for p in range(1, 16):
        total = total + pays[p]
    for b0 in range(2):
        for b1 in range(2):
            part = [pays[(b0 + 2 * b1 + 4 * b2) * NH + h] for b2 in range(2) for h in range(NH)]
            v = (part[0] + part[1]) + (part[2] + part[3])
            for i in range(3):
                row = 96 * b0 + 48 * b1 + 16 * i
                column[row : row + 16] = v[:, 96 * i : 96 * i + 96]
    for i in range(6):
        pivot[i // 2, 16 * (i % 2) : 16 * (i % 2) + 16] = total[:, 288 + 32 * i : 320 + 32 * i]


def local(factor_cols, ancestor_inverse, pivot_inverse, structure, widths, pole_weights):
    structure = structure.T

    def over_grid(v, perm):
        return lax.ppermute(v, "grid", perm)

    block = sds((ROWS, 2 * HC), BF16)
    keep, send = call(
        prep_kernel,
        [block, block],
        [(structure, "p"), (widths, "p"), (factor_cols[0], "p")],
        "prep",
        flops=2 * 2 * ROWS * HB * HB,
        scratch=[
            pltpu.SMEM(structure.shape, jnp.int32),
            pltpu.SMEM(widths.shape, jnp.int32),
            pltpu.VMEM(factor_cols.shape[1:], BF16),
            pltpu.SemaphoreType.DMA((3,)),
        ],
    )
    a_own = ancestor_inverse[0].reshape(2 * ROWS, -1)
    a_sib = over_grid(a_own, CORE)
    got_mine = over_grid(send, CORE)
    got_mine, a_sib = lax.optimization_barrier((got_mine, a_sib))
    got_theirs = over_grid(keep, CORE)

    def first(v):
        return [over_grid(v, perm) for perm in (FROM_AHEAD, FROM_BEHIND, FROM_Y)]

    def second(ahead, behind, beside):
        return [over_grid(ahead, FROM_AHEAD), over_grid(beside, FROM_BEHIND), over_grid(ahead, FROM_Y)]

    def add(old, offsets, us, vs):
        n = len(offsets)
        ins = ([] if old is None else [(old, "v")]) + [(a, "h") for a in (a_own, a_sib)]
        ins += [(b, "h") for b in (*us, *vs)]
        return call(
            functools.partial(acc_kernel, offsets, old is not None),
            [sds((2, ROWS, 2 * HC), F32)],
            ins,
            "product",
            flops=2 * n * 4 * ROWS * 2 * ROWS * 2 * HC,
            scratch=[
                pltpu.VMEM((n, 4 * ROWS, 2 * ROWS), BF16),
                pltpu.VMEM((n, 2 * ROWS, 2 * HC), BF16),
                pltpu.SemaphoreType.DMA((4 * n,)),
            ],
        )[0]

    v1 = first(got_mine)
    u1 = first(keep)
    v2 = second(*v1)
    acc = add(None, [(0, 0)], [keep], [got_mine])
    big, small = call(
        left_kernel,
        [sds((4 * HB, 2 * ROWS), BF16)] * 2,
        [(widths, "s"), (keep, "v"), (send, "v"), (got_mine, "v"), (got_theirs, "v")],
        "left",
        flops=2 * 2 * 2 * ROWS * HB * HB,
    )
    *u1, acc, big, small = lax.optimization_barrier((*u1, acc, big, small))
    u2 = second(*u1)
    acc = add(acc, [(1, 0), (-1, 0), (0, 1)], u1, v1)
    v3 = over_grid(v2[0], FROM_Y)
    *u2, acc = lax.optimization_barrier((*u2, acc))
    u3 = over_grid(u2[1], FROM_BEHIND)
    acc = add(acc, [(2, 0), (-1, 1), (1, 1)], u2, v2)
    own, sib, q = call(
        column_kernel,
        [sds((ROWS, 2 * HC), F32)] * 2 + [sds((16, 32, BIG + HB), F32)],
        [
            (structure, "s"),
            (widths, "s"),
            (acc, "v"),
            (a_own, "h"),
            (a_sib, "h"),
            (u3, "h"),
            (v3, "h"),
            (big, "h"),
            (small, "h"),
        ],
        "column",
        flops=2 * 4 * ROWS * 2 * ROWS * 2 * HC + 2 * 2 * 1024 * 2 * ROWS * 768,
        scratch=[
            pltpu.VMEM((1, 4 * ROWS, 2 * ROWS), BF16),
            pltpu.VMEM((1, 2 * ROWS, 2 * HC), BF16),
            pltpu.VMEM((4 * HB, 2 * ROWS), BF16),
            pltpu.VMEM((4 * HB, 2 * ROWS), BF16),
            pltpu.VMEM((4 * ROWS, 2 * HC), BF16),
            pltpu.VMEM((ROWS, 2 * HC), F32),
            pltpu.VMEM((ROWS, 2 * HC), F32),
            pltpu.VMEM((16, 32, BIG + HB), F32),
            pltpu.SemaphoreType.DMA((4,)),
            pltpu.SemaphoreType.DMA((6,)),
        ],
        limit=20,
        out_space=pltpu.HBM,
    )
    other = over_grid(sib, CORE)
    sums = lax.all_to_all(q, "grid", 0, 0, tiled=True)
    d_keep, d_send = call(
        term_kernel,
        [sds((96, 768), F32)] * 2,
        [(pole_weights, "s"), (own, "v"), (other, "v")],
        "term",
        scratch=[pltpu.VMEM((ROWS, 768), F32)],
    )
    d_got = lax.ppermute(d_send, "pole", z_pair(1))
    column_inverse = call(
        spread_kernel,
        [sds((2, ROWS, 3 * BIG), BF16)],
        [(widths, "s"), (own, "v"), (other, "v")],
        "spread",
    )[0]
    d_got, column_inverse = lax.optimization_barrier((d_got, column_inverse))
    d_keep, d_send = call(
        second_kernel,
        [sds((48, 768), F32)] * 2,
        [(d_keep, "v"), (d_got, "v")],
        "second",
        scratch=[pltpu.VMEM((96, 768), F32)],
    )
    d_got = lax.ppermute(d_send, "pole", z_pair(2))
    sums, d_keep = lax.optimization_barrier((sums, d_keep))
    pivot_block, pay = call(
        pivot_kernel,
        [sds((2, 3, 32, BIG), F32), sds((16, 16, 512), F32)],
        [
            (widths, "s"),
            (pole_weights, "s"),
            (pivot_inverse[0], "v"),
            (sums, "v"),
            (d_keep, "v"),
            (d_got, "v"),
        ],
        "pivot",
        scratch=[pltpu.VMEM((96, BIG), F32), pltpu.VMEM((48, 3 * BIG), F32)],
    )
    pays = lax.all_to_all(pay, "pole", 0, 0, tiled=True)
    density_column, density_pivot = call(
        density_kernel, [sds((ROWS, 96), F32), sds((3, 32, 32), F32)], [(pays, "v")], "density"
    )
    return (column_inverse[None], pivot_block[None], density_column, density_pivot)


def solution(mesh):
    in_specs = (
        P("pole", None, "grid", None),
        P("pole", None, "grid", None),
        P("pole", None, None, "grid", None),
        P(),
        P(),
        P("pole", None),
    )
    out_specs = (
        P("pole", None, "grid", None),
        P("pole", None, None, "grid", None),
        P("grid", "pole"),
        P(None, "grid", "pole"),
    )
    return jax.shard_map(local, mesh=mesh, in_specs=in_specs, out_specs=out_specs, check_vma=False)
```

```python
import functools

import jax
import jax.numpy as jnp
from jax import lax
from jax.experimental import pallas as pl
from jax.experimental.pallas import tpu as pltpu
from jax.sharding import PartitionSpec as P

F32 = jnp.float32
BF16 = jnp.bfloat16
BIG = 512
ROWS = 192
HB = 256
HS = 128
HC = HB + HS

NX, NY, NCORE = 4, 2, 2
NZ, NH = 8, 2


def grid_perm(source):
    def at(y, x, c):
        return (y * NX + x % NX) * NCORE + c

    return [
        (at(*source(y, x, c)), at(y, x, c)) for y in range(NY) for x in range(NX) for c in range(NCORE)
    ]


CORE = grid_perm(lambda y, x, c: (y, x, 1 - c))
FROM_AHEAD = grid_perm(lambda y, x, c: (y, x + 1 - 2 * c, c))
FROM_BEHIND = grid_perm(lambda y, x, c: (y, x - 1 + 2 * c, c))
FROM_FAR = grid_perm(lambda y, x, c: (y, x + 2, c))
FROM_Y = grid_perm(lambda y, x, c: (1 - y, x, c))


def pole_perm(source):
    def at(z, h):
        return z * NH + h

    return [(at(*source(z, h)), at(z, h)) for z in range(NZ) for h in range(NH)]


def z_pair(bit):
    return pole_perm(lambda z, h: (z ^ bit, h))


POLE_ORDER = [z * NH + h for z in (0, 5, 2, 7, 1, 4, 3, 6) for h in range(NH)]
GRID_ORDER = list(range(16))


def place():
    g = lax.axis_index("grid")
    c = lax.rem(g, 2)
    x = lax.rem(lax.div(g, 2), NX)
    y = lax.div(g, 2 * NX)
    return g, c, x, y


def z_bits():
    z = lax.div(lax.axis_index("pole"), NH)
    return lax.rem(z, 2), lax.rem(lax.div(z, 2), 2)


def supers(widths):
    kb = jnp.where(widths[0] == BIG, 0, jnp.where(widths[1] == BIG, 1, 2))
    k1 = jnp.where(kb == 0, 1, 0)
    k2 = jnp.where(kb == 2, 1, 2)
    return kb, k1, k2, widths[k1]


def iota(shape, axis):
    return lax.broadcasted_iota(jnp.int32, shape, axis)


def row_mask(structure, block, count, k, lanes):
    return jnp.concatenate(
        [jnp.full((32, lanes), structure[k, block + i].astype(F32), F32) for i in range(count)], axis=0
    )


def call(body, outs, ins, name, flops=0, scratch=(), limit=16, out_space=pltpu.VMEM):
    spaces = {"s": pltpu.SMEM, "v": pltpu.VMEM, "h": pltpu.HBM, "p": pltpu.HBM}
    size = sum(a.size * a.dtype.itemsize for a, _ in ins) + sum(
        o.size * o.dtype.itemsize for o in outs
    )
    if out_space is pltpu.HBM:
        outs = [pltpu.HBM(o.shape, o.dtype) for o in outs]
    return pl.pallas_call(
        body,
        out_shape=tuple(outs),
        in_specs=[pl.BlockSpec(memory_space=spaces[kind]) for _, kind in ins],
        out_specs=tuple(pl.BlockSpec(memory_space=out_space) for _ in outs),
        scratch_shapes=list(scratch),
        compiler_params=pltpu.CompilerParams(vmem_limit_bytes=limit * 1024 * 1024),
        cost_estimate=pl.CostEstimate(flops=flops, bytes_accessed=size, transcendentals=0),
        name=name,
    )(*[pltpu.with_memory_space_constraint(a, pltpu.HBM) if kind == "p" else a for a, kind in ins])


def sds(shape, dtype):
    return jax.ShapeDtypeStruct(shape, dtype)


def prep_kernel(structure_in, widths_in, f_in, keep, send, structure, widths, f, sems):
    pairs = ((widths_in, widths), (structure_in, structure), (f_in, f))
    copies = [pltpu.make_async_copy(v, to, sems.at[i]) for i, (v, to) in enumerate(pairs)]
    for copy in copies:
        copy.start()
    for copy in copies:
        copy.wait()
    g, c, _, _ = place()
    kb, k1, k2, a = supers(widths)
    base = g * 6
    mask_b = row_mask(structure, base, 6, kb, HB).astype(BF16)
    mask_1 = row_mask(structure, base, 6, k1, HB).astype(BF16)
    mask_2 = row_mask(structure, base, 6, k2, HB).astype(BF16)
    shift = (iota((HB, HB), 0) + a == iota((HB, HB), 1)).astype(BF16)
    first = iota((ROWS, HB), 1) < a

    def at(k, part):
        return pl.ds(pl.multiple_of(k * BIG + part * HB, HB), HB)

    for p in range(2):
        o = p * HC
        keep[:, o : o + HB] = f[p, :, at(kb, c)] * mask_b
        send[:, o : o + HB] = f[p, :, at(kb, 1 - c)] * mask_b
        one = (f[p, :, at(k1, 0)] * mask_1).astype(F32)
        two = jnp.dot(f[p, :, at(k2, 0)] * mask_2, shift, preferred_element_type=F32)
        small = jnp.where(first, one, two)
        low, high = small[:, :HS], small[:, HS:]
        keep[:, o + HB : o + HC] = jnp.where(c == 0, low, high).astype(BF16)
        send[:, o + HB : o + HC] = jnp.where(c == 0, high, low).astype(BF16)


def left_kernel(widths, keep, send, got_mine, got_theirs, big, small):
    _, c, _, _ = place()
    _, _, _, a = supers(widths)
    back = (iota((HB, HB), 0) == iota((HB, HB), 1) + a).astype(BF16)
    mine = jnp.concatenate([keep[...], got_mine[...]], axis=0)
    theirs = jnp.concatenate([send[...], got_theirs[...]], axis=0)
    for p in range(2):
        o = p * HC
        for part, half in ((c, mine), (1 - c, theirs)):
            at = pl.ds(pl.multiple_of((2 * part + p) * HB, HB), HB)
            big[at, :] = half[:, o : o + HB].astype(F32).T.astype(BF16)
        m, t = mine[:, o + HB : o + HC].astype(F32), theirs[:, o + HB : o + HC].astype(F32)
        low, high = jnp.where(c == 0, m, t), jnp.where(c == 0, t, m)
        both = jnp.concatenate([low, high], axis=1)
        moved = jnp.dot(both.astype(BF16), back, preferred_element_type=F32)
        small[p * HB : (p + 1) * HB] = both.T.astype(BF16)
        small[(2 + p) * HB : (3 + p) * HB] = moved.T.astype(BF16)


def rows_at(bit, count):
    return pl.ds(pl.multiple_of(bit * count, count), count)


def block_copies(offsets, a_own, a_sib, us, vs, left, rows, sems):
    _, c, x, y = place()
    side = 1 - 2 * c
    copies = []
    for i, (dx, dy) in enumerate(offsets):
        at = lax.rem(y + dy, NY) * NX + lax.rem(x + dx * side + NX, NX)
        cols = pl.ds(pl.multiple_of(at * 2 * ROWS, 2 * ROWS), 2 * ROWS)
        pairs = [
            (us[i], rows.at[i, rows_at(c, ROWS)]),
            (vs[i], rows.at[i, rows_at(1 - c, ROWS)]),
            (a_own.at[:, cols], left.at[i, : 2 * ROWS]),
            (a_sib.at[:, cols], left.at[i, 2 * ROWS :]),
        ]
        copies += [pltpu.make_async_copy(v, to, sems.at[4 * i + j]) for j, (v, to) in enumerate(pairs)]
    return copies


def add_blocks(copies, left, rows, get, put):
    z = None
    for i in range(len(copies) // 4):
        for copy in copies[4 * i : 4 * i + 4]:
            copy.wait()
        d = jnp.dot(left[i], rows[i], preferred_element_type=F32)
        z = d if z is None else z + d
    for s in range(2):
        re, im = z[2 * s * ROWS : (2 * s + 1) * ROWS], z[(2 * s + 1) * ROWS : (2 * s + 2) * ROWS]
        old_re, old_im = get(s)
        put(s, old_re + (re[:, :HC] - im[:, HC:]), old_im + (re[:, HC:] + im[:, :HC]))


def acc_kernel(offsets, has_acc, *refs):
    refs = list(refs)
    old = refs.pop(0) if has_acc else None
    n = len(offsets)
    a_own, a_sib, us, vs = refs[0], refs[1], refs[2 : 2 + n], refs[2 + n : 2 + 2 * n]
    out, left, rows, sems = refs[2 + 2 * n :]
    copies = block_copies(offsets, a_own, a_sib, us, vs, left, rows, sems)
    for copy in copies:
        copy.start()

    def get(s):
        if old is None:
            return 0.0, 0.0
        return old[s, :, :HC], old[s, :, HC:]

    def put(s, re, im):
        out[s, :, :HC] = re
        out[s, :, HC:] = im

    add_blocks(copies, left, rows, get, put)


def column_kernel(structure, widths, old, a_own, a_sib, u, v, big_in, small_in, own_out, sib_out, q_out, *scratch):
    left, rows, big, small, gs, own, sib, q, sems, in_sems = scratch
    g, c, _, _ = place()
    kb, k1, k2, a = supers(widths)

    def get(s):
        return old[s, :, :HC], old[s, :, HC:]

    def put(s, re, im):
        base = (g + s * (1 - 2 * c)) * 6
        mask_b = row_mask(structure, base, 6, kb, HB)
        mask_1 = row_mask(structure, base, 6, k1, HS)
        mask_2 = row_mask(structure, base, 6, k2, HS)
        mask_s = jnp.where(iota((ROWS, HS), 1) + c * HS < a, mask_1, mask_2)
        out = own if s == 0 else sib
        for p, w in ((0, re), (1, im)):
            vb = -(w[:, :HB] * mask_b)
            vs = -(w[:, HB:] * mask_s)
            out[:, p * HC : p * HC + HB] = vb
            out[:, p * HC + HB : (p + 1) * HC] = vs
            for part, lo, hi in ((vb, p * HB, (p + 1) * HB), (vs, 2 * HB + p * HS, 2 * HB + (p + 1) * HS)):
                top = part.astype(BF16)
                gs[s * ROWS : (s + 1) * ROWS, lo:hi] = top
                gs[(s + 2) * ROWS : (s + 3) * ROWS, lo:hi] = (part - top.astype(F32)).astype(BF16)

    blocks = block_copies([(2, 1)], a_own, a_sib, [u], [v], left, rows, in_sems)
    lefts = [
        pltpu.make_async_copy(big_in, big, in_sems.at[4]),
        pltpu.make_async_copy(small_in, small, in_sems.at[5]),
    ]
    for copy in blocks + lefts:
        copy.start()
    add_blocks(blocks, left, rows, get, put)
    copies = [pltpu.make_async_copy(sib, sib_out, sems.at[0]), pltpu.make_async_copy(own, own_out, sems.at[1])]
    for copy in copies:
        copy.start()

    def across(left, lo, hi):
        twice = jnp.concatenate([left[...], left[...]], axis=1)
        return jnp.dot(twice, gs[:, lo:hi], preferred_element_type=F32)

    lefts[0].wait()
    z = across(big, 0, BIG)
    for h in range(2):
        re, im = z[2 * h * HB : (2 * h + 1) * HB], z[(2 * h + 1) * HB : (2 * h + 2) * HB]
        for t in range(8):
            r = slice(32 * t, 32 * t + 32)
            to = GRID_ORDER.index(8 * h + t)
            q[to, :, :HB] = re[r, :HB] - im[r, HB:]
            q[to, :, HB:BIG] = re[r, HB:] + im[r, :HB]
    copies.append(pltpu.make_async_copy(q.at[:, :, :BIG], q_out.at[:, :, :BIG], sems.at[2]))
    copies[2].start()
    lefts[1].wait()
    z = across(small, BIG, BIG + HB)
    col = iota((HB, HS), 1) + c * HS
    row = iota((HB, HS), 0)
    parts = []
    for i in range(2):
        re, im = z[2 * i * HB : (2 * i + 1) * HB], z[(2 * i + 1) * HB : (2 * i + 2) * HB]
        parts.append((re[:, :HS] - im[:, HS:], re[:, HS:] + im[:, :HS]))
    for p in range(2):
        e = jnp.where(
            col < a, jnp.where(row < a, parts[0][p], 0.0), jnp.where(row < HB - a, parts[1][p], 0.0)
        )
        at = slice(BIG + p * HS, BIG + (p + 1) * HS)
        for t in range(8):
            q[GRID_ORDER.index(t), :, at] = e[32 * t : 32 * t + 32]
            q[GRID_ORDER.index(8 + t), :, at] = jnp.zeros((32, HS), F32)
    copies.append(pltpu.make_async_copy(q.at[:, :, BIG:], q_out.at[:, :, BIG:], sems.at[3]))
    copies[3].start()
    for copy in copies:
        copy.wait()


def halves_of(mine, other):
    return [
        [(ref[:, p * HC : p * HC + HB], ref[:, p * HC + HB : (p + 1) * HC]) for p in range(2)]
        for ref in (mine, other)
    ]


def in_order(c, first, second):
    return jnp.concatenate([jnp.where(c == 0, first, second), jnp.where(c == 0, second, first)], axis=1)


def term_kernel(weights, mine, other, keep, send, wide):
    _, c, _, _ = place()
    odd, _ = z_bits()
    wr, wi = weights[0, 0], weights[0, 1]
    m, t = ([wr * half[1][i] + wi * half[0][i] for i in range(2)] for half in halves_of(mine, other))
    wide[:, :BIG] = in_order(c, m[0], t[0])
    wide[:, BIG:] = in_order(c, m[1], t[1])
    keep[...] = wide[rows_at(odd, 96), :]
    send[...] = wide[rows_at(1 - odd, 96), :]


def spread_kernel(widths, mine, other, out):
    _, c, _, _ = place()
    kb, k1, k2, a = supers(widths)
    back = (iota((HB, HB), 0) == iota((HB, HB), 1) + a).astype(BF16)
    lane = iota((ROWS, HB), 1)

    def at(k, part):
        return pl.ds(pl.multiple_of(k * BIG + part * HB, HB), HB)

    zero = jnp.zeros((ROWS, HB), BF16)
    halves = halves_of(mine, other)
    for p in range(2):
        m, t = halves[0][p], halves[1][p]
        out[p, :, at(kb, c)] = m[0].astype(BF16)
        out[p, :, at(kb, 1 - c)] = t[0].astype(BF16)
        s = in_order(c, m[1], t[1])
        out[p, :, at(k1, 0)] = jnp.where(lane < a, s, 0.0).astype(BF16)
        out[p, :, at(k1, 1)] = zero
        out[p, :, at(k2, 0)] = jnp.dot(s.astype(BF16), back, preferred_element_type=F32).astype(BF16)
        out[p, :, at(k2, 1)] = zero


def second_kernel(old, got, keep, send, total):
    _, bit = z_bits()
    total[...] = old[...] + got[...]
    keep[...] = total[rows_at(bit, 48), :]
    send[...] = total[rows_at(1 - bit, 48), :]


def pivot_kernel(widths, weights, pivot, sums, keep, got, block, pay, wide, column):
    g = lax.axis_index("grid")
    kb, k1, k2, a = supers(widths)
    wr, wi = weights[0, 0], weights[0, 1]
    parts = [[sums[GRID_ORDER.index(2 * i + core)] for i in range(8)] for core in range(2)]
    m, t = (functools.reduce(lambda u, v: u + v, part) for part in parts)
    row = iota((32, BIG), 0) + g * 32
    line = iota((32, BIG), 1)
    blank = jnp.zeros((32, HB), F32)
    q = []
    for p in range(2):
        full = jnp.concatenate([u[:, p * HB : (p + 1) * HB] for u in (m, t)], axis=1)
        e = jnp.concatenate([u[:, BIG + p * HS : BIG + (p + 1) * HS] for u in (m, t)], axis=1)
        moved = pltpu.roll(e, HB - a, 1)
        q.append((full, jnp.concatenate([e, blank], axis=1), jnp.concatenate([moved, blank], axis=1)))
    for i, (k, w) in enumerate(((kb, BIG), (k1, a), (k2, HB - a))):
        live = (row < w) & (line < w)
        blocks = []
        for p in range(2):
            b = jnp.where(live, pivot[p, k] - q[p][i], 0.0)
            block[p, k] = b
            blocks.append(b)
        wide[pl.ds(pl.multiple_of(k * 32, 32), 32), :] = wr * blocks[1] + wi * blocks[0]
    d = keep[...] + got[...]
    lane = iota((48, HB), 1)
    small = d[:, BIG:]
    none = jnp.zeros((48, HB), F32)

    def at(k, part):
        return pl.ds(pl.multiple_of(k * BIG + part * HB, HB), HB)

    for part in range(2):
        column[:, at(kb, part)] = d[:, part * HB : (part + 1) * HB]
    column[:, at(k1, 0)] = jnp.where(lane < a, small, 0.0)
    column[:, at(k1, 1)] = none
    column[:, at(k2, 0)] = jnp.where(lane < HB - a, pltpu.roll(small, HB - a, 1), 0.0)
    column[:, at(k2, 1)] = none
    v, w = column[...], wide[...]
    pad = jnp.zeros((16, 32), F32)
    for j, p in enumerate(POLE_ORDER):
        parts = [v[16 * i : 16 * i + 16, 96 * p : 96 * p + 96] for i in range(3)]
        parts += [w[16 * i : 16 * i + 16, 32 * p : 32 * p + 32] for i in range(6)]
        pay[j] = jnp.concatenate(parts + [pad], axis=1)


def density_kernel(pays, column, pivot):
    total = pays[0]
    for p in range(1, 16):
        total = total + pays[p]
    for b0 in range(2):
        for b1 in range(2):
            part = [pays[POLE_ORDER.index((b0 + 2 * b1 + 4 * b2) * NH + h)] for b2 in range(2) for h in range(NH)]
            v = (part[0] + part[1]) + (part[2] + part[3])
            for i in range(3):
                row = 96 * b0 + 48 * b1 + 16 * i
                column[row : row + 16] = v[:, 96 * i : 96 * i + 96]
    for i in range(6):
        pivot[i // 2, 16 * (i % 2) : 16 * (i % 2) + 16] = total[:, 288 + 32 * i : 320 + 32 * i]


def local(factor_cols, ancestor_inverse, pivot_inverse, structure, widths, pole_weights):
    structure = structure.T

    def over_grid(v, perm):
        return lax.ppermute(v, "grid", perm)

    block = sds((ROWS, 2 * HC), BF16)
    keep, send = call(
        prep_kernel,
        [block, block],
        [(structure, "p"), (widths, "p"), (factor_cols[0], "p")],
        "prep",
        flops=2 * 2 * ROWS * HB * HB,
        scratch=[
            pltpu.SMEM(structure.shape, jnp.int32),
            pltpu.SMEM(widths.shape, jnp.int32),
            pltpu.VMEM(factor_cols.shape[1:], BF16),
            pltpu.SemaphoreType.DMA((3,)),
        ],
    )
    a_own = ancestor_inverse[0].reshape(2 * ROWS, -1)
    a_sib = over_grid(a_own, CORE)
    got_mine = over_grid(send, CORE)
    got_mine, a_sib = lax.optimization_barrier((got_mine, a_sib))
    got_theirs = over_grid(keep, CORE)

    def first(v):
        return [over_grid(v, perm) for perm in (FROM_AHEAD, FROM_BEHIND, FROM_Y)]

    def second(ahead, behind, beside):
        return [over_grid(ahead, FROM_AHEAD), over_grid(beside, FROM_BEHIND), over_grid(ahead, FROM_Y)]

    def add(old, offsets, us, vs):
        n = len(offsets)
        ins = ([] if old is None else [(old, "v")]) + [(a, "h") for a in (a_own, a_sib)]
        ins += [(b, "h") for b in (*us, *vs)]
        return call(
            functools.partial(acc_kernel, offsets, old is not None),
            [sds((2, ROWS, 2 * HC), F32)],
            ins,
            "product",
            flops=2 * n * 4 * ROWS * 2 * ROWS * 2 * HC,
            scratch=[
                pltpu.VMEM((n, 4 * ROWS, 2 * ROWS), BF16),
                pltpu.VMEM((n, 2 * ROWS, 2 * HC), BF16),
                pltpu.SemaphoreType.DMA((4 * n,)),
            ],
        )[0]

    v1 = first(got_mine)
    u1 = first(keep)
    v2 = second(*v1)
    acc = add(None, [(0, 0)], [keep], [got_mine])
    big, small = call(
        left_kernel,
        [sds((4 * HB, 2 * ROWS), BF16)] * 2,
        [(widths, "s"), (keep, "v"), (send, "v"), (got_mine, "v"), (got_theirs, "v")],
        "left",
        flops=2 * 2 * 2 * ROWS * HB * HB,
    )
    *u1, acc, big, small = lax.optimization_barrier((*u1, acc, big, small))
    u2 = second(*u1)
    acc = add(acc, [(1, 0), (-1, 0), (0, 1)], u1, v1)
    v3 = over_grid(v2[0], FROM_Y)
    *u2, acc = lax.optimization_barrier((*u2, acc))
    u3 = over_grid(u2[1], FROM_BEHIND)
    acc = add(acc, [(2, 0), (-1, 1), (1, 1)], u2, v2)
    own, sib, q = call(
        column_kernel,
        [sds((ROWS, 2 * HC), F32)] * 2 + [sds((16, 32, BIG + HB), F32)],
        [
            (structure, "s"),
            (widths, "s"),
            (acc, "v"),
            (a_own, "h"),
            (a_sib, "h"),
            (u3, "h"),
            (v3, "h"),
            (big, "h"),
            (small, "h"),
        ],
        "column",
        flops=2 * 4 * ROWS * 2 * ROWS * 2 * HC + 2 * 2 * 1024 * 2 * ROWS * 768,
        scratch=[
            pltpu.VMEM((1, 4 * ROWS, 2 * ROWS), BF16),
            pltpu.VMEM((1, 2 * ROWS, 2 * HC), BF16),
            pltpu.VMEM((4 * HB, 2 * ROWS), BF16),
            pltpu.VMEM((4 * HB, 2 * ROWS), BF16),
            pltpu.VMEM((4 * ROWS, 2 * HC), BF16),
            pltpu.VMEM((ROWS, 2 * HC), F32),
            pltpu.VMEM((ROWS, 2 * HC), F32),
            pltpu.VMEM((16, 32, BIG + HB), F32),
            pltpu.SemaphoreType.DMA((4,)),
            pltpu.SemaphoreType.DMA((6,)),
        ],
        limit=20,
        out_space=pltpu.HBM,
    )
    other = over_grid(sib, CORE)
    sums = lax.all_to_all(q, "grid", 0, 0, axis_index_groups=[GRID_ORDER], tiled=True)
    d_keep, d_send = call(
        term_kernel,
        [sds((96, 768), F32)] * 2,
        [(pole_weights, "s"), (own, "v"), (other, "v")],
        "term",
        scratch=[pltpu.VMEM((ROWS, 768), F32)],
    )
    d_got = lax.ppermute(d_send, "pole", z_pair(1))
    column_inverse = call(
        spread_kernel,
        [sds((2, ROWS, 3 * BIG), BF16)],
        [(widths, "s"), (own, "v"), (other, "v")],
        "spread",
    )[0]
    d_got, column_inverse = lax.optimization_barrier((d_got, column_inverse))
    d_keep, d_send = call(
        second_kernel,
        [sds((48, 768), F32)] * 2,
        [(d_keep, "v"), (d_got, "v")],
        "second",
        scratch=[pltpu.VMEM((96, 768), F32)],
    )
    d_got = lax.ppermute(d_send, "pole", z_pair(2))
    sums, d_keep = lax.optimization_barrier((sums, d_keep))
    pivot_block, pay = call(
        pivot_kernel,
        [sds((2, 3, 32, BIG), F32), sds((16, 16, 512), F32)],
        [
            (widths, "s"),
            (pole_weights, "s"),
            (pivot_inverse[0], "v"),
            (sums, "v"),
            (d_keep, "v"),
            (d_got, "v"),
        ],
        "pivot",
        scratch=[pltpu.VMEM((96, BIG), F32), pltpu.VMEM((48, 3 * BIG), F32)],
    )
    pays = lax.all_to_all(pay, "pole", 0, 0, axis_index_groups=[POLE_ORDER], tiled=True)
    density_column, density_pivot = call(
        density_kernel, [sds((ROWS, 96), F32), sds((3, 32, 32), F32)], [(pays, "v")], "density"
    )
    return (column_inverse[None], pivot_block[None], density_column, density_pivot)


def solution(mesh):
    in_specs = (
        P("pole", None, "grid", None),
        P("pole", None, "grid", None),
        P("pole", None, None, "grid", None),
        P(),
        P(),
        P("pole", None),
    )
    out_specs = (
        P("pole", None, "grid", None),
        P("pole", None, None, "grid", None),
        P("grid", "pole"),
        P(None, "grid", "pole"),
    )
    return jax.shard_map(local, mesh=mesh, in_specs=in_specs, out_specs=out_specs, check_vma=False)
```

```python
import functools

import jax
import jax.numpy as jnp
from jax import lax
from jax.experimental import pallas as pl
from jax.experimental.pallas import tpu as pltpu
from jax.sharding import PartitionSpec as P

F32 = jnp.float32
BF16 = jnp.bfloat16
BIG = 512
ROWS = 192
HB = 256
HS = 128
HC = HB + HS

NX, NY, NCORE = 4, 2, 2
NZ, NH = 8, 2


def grid_perm(source):
    def at(y, x, c):
        return (y * NX + x % NX) * NCORE + c

    return [
        (at(*source(y, x, c)), at(y, x, c)) for y in range(NY) for x in range(NX) for c in range(NCORE)
    ]


CORE = grid_perm(lambda y, x, c: (y, x, 1 - c))
FROM_AHEAD = grid_perm(lambda y, x, c: (y, x + 1 - 2 * c, c))
FROM_BEHIND = grid_perm(lambda y, x, c: (y, x - 1 + 2 * c, c))
FROM_FAR = grid_perm(lambda y, x, c: (y, x + 2, c))
FROM_Y = grid_perm(lambda y, x, c: (1 - y, x, c))


def z_pair(bit):
    def at(z, h, g):
        return ((z % NZ) * NH + h) * NX * NY * NCORE + g

    return [
        (at((((z - g % NCORE) % NZ) ^ bit) + g % NCORE, h, g), at(z, h, g))
        for z in range(NZ)
        for h in range(NH)
        for g in range(NX * NY * NCORE)
    ]


POLE_ORDER = [z * NH + h for z in (0, 5, 2, 7, 1, 4, 3, 6) for h in range(NH)]
GRID_ORDER = [(y * NX + x) * NCORE + c for x in (0, 2, 1, 3) for y in range(NY) for c in range(NCORE)]


def place():
    g = lax.axis_index("grid")
    c = lax.rem(g, 2)
    x = lax.rem(lax.div(g, 2), NX)
    y = lax.div(g, 2 * NX)
    return g, c, x, y


def z_bits():
    z = lax.div(lax.axis_index("pole"), NH)
    z = lax.rem(z + NZ - lax.rem(lax.axis_index("grid"), NCORE), NZ)
    return lax.rem(z, 2), lax.rem(lax.div(z, 2), 2)


def supers(widths):
    kb = jnp.where(widths[0] == BIG, 0, jnp.where(widths[1] == BIG, 1, 2))
    k1 = jnp.where(kb == 0, 1, 0)
    k2 = jnp.where(kb == 2, 1, 2)
    return kb, k1, k2, widths[k1]


def iota(shape, axis):
    return lax.broadcasted_iota(jnp.int32, shape, axis)


def row_mask(structure, block, count, k, lanes):
    return jnp.concatenate(
        [jnp.full((32, lanes), structure[k, block + i].astype(F32), F32) for i in range(count)], axis=0
    )


def call(body, outs, ins, name, flops=0, scratch=(), limit=16, out_space=pltpu.VMEM):
    spaces = {"s": pltpu.SMEM, "v": pltpu.VMEM, "h": pltpu.HBM, "p": pltpu.HBM}
    size = sum(a.size * a.dtype.itemsize for a, _ in ins) + sum(
        o.size * o.dtype.itemsize for o in outs
    )
    if out_space is pltpu.HBM:
        outs = [pltpu.HBM(o.shape, o.dtype) for o in outs]
    return pl.pallas_call(
        body,
        out_shape=tuple(outs),
        in_specs=[pl.BlockSpec(memory_space=spaces[kind]) for _, kind in ins],
        out_specs=tuple(pl.BlockSpec(memory_space=out_space) for _ in outs),
        scratch_shapes=list(scratch),
        compiler_params=pltpu.CompilerParams(vmem_limit_bytes=limit * 1024 * 1024),
        cost_estimate=pl.CostEstimate(flops=flops, bytes_accessed=size, transcendentals=0),
        name=name,
    )(*[pltpu.with_memory_space_constraint(a, pltpu.HBM) if kind == "p" else a for a, kind in ins])


def sds(shape, dtype):
    return jax.ShapeDtypeStruct(shape, dtype)


def prep_kernel(structure_in, widths_in, f_in, keep, send, structure, widths, f, sems):
    pairs = ((widths_in, widths), (structure_in, structure), (f_in, f))
    copies = [pltpu.make_async_copy(v, to, sems.at[i]) for i, (v, to) in enumerate(pairs)]
    for copy in copies:
        copy.start()
    for copy in copies:
        copy.wait()
    g, c, _, _ = place()
    kb, k1, k2, a = supers(widths)
    base = g * 6
    mask_b = row_mask(structure, base, 6, kb, HB).astype(BF16)
    mask_1 = row_mask(structure, base, 6, k1, HB).astype(BF16)
    mask_2 = row_mask(structure, base, 6, k2, HB).astype(BF16)
    shift = (iota((HB, HB), 0) + a == iota((HB, HB), 1)).astype(BF16)
    first = iota((ROWS, HB), 1) < a

    def at(k, part):
        return pl.ds(pl.multiple_of(k * BIG + part * HB, HB), HB)

    for p in range(2):
        o = p * HC
        keep[:, o : o + HB] = f[p, :, at(kb, c)] * mask_b
        send[:, o : o + HB] = f[p, :, at(kb, 1 - c)] * mask_b
        one = (f[p, :, at(k1, 0)] * mask_1).astype(F32)
        two = jnp.dot(f[p, :, at(k2, 0)] * mask_2, shift, preferred_element_type=F32)
        small = jnp.where(first, one, two)
        low, high = small[:, :HS], small[:, HS:]
        keep[:, o + HB : o + HC] = jnp.where(c == 0, low, high).astype(BF16)
        send[:, o + HB : o + HC] = jnp.where(c == 0, high, low).astype(BF16)


def left_kernel(widths, keep, send, got_mine, got_theirs, big, small):
    _, c, _, _ = place()
    _, _, _, a = supers(widths)
    back = (iota((HB, HB), 0) == iota((HB, HB), 1) + a).astype(BF16)
    mine = jnp.concatenate([keep[...], got_mine[...]], axis=0)
    theirs = jnp.concatenate([send[...], got_theirs[...]], axis=0)
    for p in range(2):
        o = p * HC
        for part, half in ((c, mine), (1 - c, theirs)):
            at = pl.ds(pl.multiple_of((2 * part + p) * HB, HB), HB)
            big[at, :] = half[:, o : o + HB].astype(F32).T.astype(BF16)
        m, t = mine[:, o + HB : o + HC].astype(F32), theirs[:, o + HB : o + HC].astype(F32)
        low, high = jnp.where(c == 0, m, t), jnp.where(c == 0, t, m)
        both = jnp.concatenate([low, high], axis=1)
        moved = jnp.dot(both.astype(BF16), back, preferred_element_type=F32)
        small[p * HB : (p + 1) * HB] = both.T.astype(BF16)
        small[(2 + p) * HB : (3 + p) * HB] = moved.T.astype(BF16)


def rows_at(bit, count):
    return pl.ds(pl.multiple_of(bit * count, count), count)


def block_copies(offsets, a_own, a_sib, us, vs, left, rows, sems):
    _, c, x, y = place()
    side = 1 - 2 * c
    copies = []
    for i, (dx, dy) in enumerate(offsets):
        at = lax.rem(y + dy, NY) * NX + lax.rem(x + dx * side + NX, NX)
        cols = pl.ds(pl.multiple_of(at * 2 * ROWS, 2 * ROWS), 2 * ROWS)
        pairs = [
            (us[i], rows.at[i, rows_at(c, ROWS)]),
            (vs[i], rows.at[i, rows_at(1 - c, ROWS)]),
            (a_own.at[:, cols], left.at[i, : 2 * ROWS]),
            (a_sib.at[:, cols], left.at[i, 2 * ROWS :]),
        ]
        copies += [pltpu.make_async_copy(v, to, sems.at[4 * i + j]) for j, (v, to) in enumerate(pairs)]
    return copies


def add_blocks(copies, left, rows, get, put):
    z = None
    for i in range(len(copies) // 4):
        for copy in copies[4 * i : 4 * i + 4]:
            copy.wait()
        d = jnp.dot(left[i], rows[i], preferred_element_type=F32)
        z = d if z is None else z + d
    for s in range(2):
        re, im = z[2 * s * ROWS : (2 * s + 1) * ROWS], z[(2 * s + 1) * ROWS : (2 * s + 2) * ROWS]
        old_re, old_im = get(s)
        put(s, old_re + (re[:, :HC] - im[:, HC:]), old_im + (re[:, HC:] + im[:, :HC]))


def acc_kernel(offsets, has_acc, *refs):
    refs = list(refs)
    old = refs.pop(0) if has_acc else None
    n = len(offsets)
    a_own, a_sib, us, vs = refs[0], refs[1], refs[2 : 2 + n], refs[2 + n : 2 + 2 * n]
    out, left, rows, sems = refs[2 + 2 * n :]
    copies = block_copies(offsets, a_own, a_sib, us, vs, left, rows, sems)
    for copy in copies:
        copy.start()

    def get(s):
        if old is None:
            return 0.0, 0.0
        return old[s, :, :HC], old[s, :, HC:]

    def put(s, re, im):
        out[s, :, :HC] = re
        out[s, :, HC:] = im

    add_blocks(copies, left, rows, get, put)


def column_kernel(structure, widths, old, a_own, a_sib, u, v, big_in, small_in, own_out, sib_out, q_out, *scratch):
    left, rows, big, small, gs, own, sib, q, sems, in_sems = scratch
    g, c, _, _ = place()
    kb, k1, k2, a = supers(widths)

    def get(s):
        return old[s, :, :HC], old[s, :, HC:]

    def put(s, re, im):
        base = (g + s * (1 - 2 * c)) * 6
        mask_b = row_mask(structure, base, 6, kb, HB)
        mask_1 = row_mask(structure, base, 6, k1, HS)
        mask_2 = row_mask(structure, base, 6, k2, HS)
        mask_s = jnp.where(iota((ROWS, HS), 1) + c * HS < a, mask_1, mask_2)
        out = own if s == 0 else sib
        for p, w in ((0, re), (1, im)):
            vb = -(w[:, :HB] * mask_b)
            vs = -(w[:, HB:] * mask_s)
            out[:, p * HC : p * HC + HB] = vb
            out[:, p * HC + HB : (p + 1) * HC] = vs
            for part, lo, hi in ((vb, p * HB, (p + 1) * HB), (vs, 2 * HB + p * HS, 2 * HB + (p + 1) * HS)):
                top = part.astype(BF16)
                gs[s * ROWS : (s + 1) * ROWS, lo:hi] = top
                gs[(s + 2) * ROWS : (s + 3) * ROWS, lo:hi] = (part - top.astype(F32)).astype(BF16)

    blocks = block_copies([(2, 1)], a_own, a_sib, [u], [v], left, rows, in_sems)
    lefts = [
        pltpu.make_async_copy(big_in, big, in_sems.at[4]),
        pltpu.make_async_copy(small_in, small, in_sems.at[5]),
    ]
    for copy in blocks + lefts:
        copy.start()
    add_blocks(blocks, left, rows, get, put)
    copies = [pltpu.make_async_copy(sib, sib_out, sems.at[0]), pltpu.make_async_copy(own, own_out, sems.at[1])]
    for copy in copies:
        copy.start()

    def across(left, lo, hi):
        twice = jnp.concatenate([left[...], left[...]], axis=1)
        return jnp.dot(twice, gs[:, lo:hi], preferred_element_type=F32)

    lefts[0].wait()
    z = across(big, 0, BIG)
    for h in range(2):
        re, im = z[2 * h * HB : (2 * h + 1) * HB], z[(2 * h + 1) * HB : (2 * h + 2) * HB]
        for t in range(8):
            r = slice(32 * t, 32 * t + 32)
            to = GRID_ORDER.index(8 * h + t)
            q[to, :, :HB] = re[r, :HB] - im[r, HB:]
            q[to, :, HB:BIG] = re[r, HB:] + im[r, :HB]
    copies.append(pltpu.make_async_copy(q.at[:, :, :BIG], q_out.at[:, :, :BIG], sems.at[2]))
    copies[2].start()
    lefts[1].wait()
    z = across(small, BIG, BIG + HB)
    col = iota((HB, HS), 1) + c * HS
    row = iota((HB, HS), 0)
    parts = []
    for i in range(2):
        re, im = z[2 * i * HB : (2 * i + 1) * HB], z[(2 * i + 1) * HB : (2 * i + 2) * HB]
        parts.append((re[:, :HS] - im[:, HS:], re[:, HS:] + im[:, :HS]))
    for p in range(2):
        e = jnp.where(
            col < a, jnp.where(row < a, parts[0][p], 0.0), jnp.where(row < HB - a, parts[1][p], 0.0)
        )
        at = slice(BIG + p * HS, BIG + (p + 1) * HS)
        for t in range(8):
            q[GRID_ORDER.index(t), :, at] = e[32 * t : 32 * t + 32]
            q[GRID_ORDER.index(8 + t), :, at] = jnp.zeros((32, HS), F32)
    copies.append(pltpu.make_async_copy(q.at[:, :, BIG:], q_out.at[:, :, BIG:], sems.at[3]))
    copies[3].start()
    for copy in copies:
        copy.wait()


def halves_of(mine, other):
    return [
        [(ref[:, p * HC : p * HC + HB], ref[:, p * HC + HB : (p + 1) * HC]) for p in range(2)]
        for ref in (mine, other)
    ]


def in_order(c, first, second):
    return jnp.concatenate([jnp.where(c == 0, first, second), jnp.where(c == 0, second, first)], axis=1)


def term_kernel(weights, mine, other, keep, send, wide):
    _, c, _, _ = place()
    odd, _ = z_bits()
    wr, wi = weights[0, 0], weights[0, 1]
    m, t = ([wr * half[1][i] + wi * half[0][i] for i in range(2)] for half in halves_of(mine, other))
    wide[:, :BIG] = in_order(c, m[0], t[0])
    wide[:, BIG:] = in_order(c, m[1], t[1])
    keep[...] = wide[rows_at(odd, 96), :]
    send[...] = wide[rows_at(1 - odd, 96), :]


def spread_kernel(widths, mine, other, out):
    _, c, _, _ = place()
    kb, k1, k2, a = supers(widths)
    back = (iota((HB, HB), 0) == iota((HB, HB), 1) + a).astype(BF16)
    lane = iota((ROWS, HB), 1)

    def at(k, part):
        return pl.ds(pl.multiple_of(k * BIG + part * HB, HB), HB)

    zero = jnp.zeros((ROWS, HB), BF16)
    halves = halves_of(mine, other)
    for p in range(2):
        m, t = halves[0][p], halves[1][p]
        out[p, :, at(kb, c)] = m[0].astype(BF16)
        out[p, :, at(kb, 1 - c)] = t[0].astype(BF16)
        s = in_order(c, m[1], t[1])
        out[p, :, at(k1, 0)] = jnp.where(lane < a, s, 0.0).astype(BF16)
        out[p, :, at(k1, 1)] = zero
        out[p, :, at(k2, 0)] = jnp.dot(s.astype(BF16), back, preferred_element_type=F32).astype(BF16)
        out[p, :, at(k2, 1)] = zero


def second_kernel(old, got, keep, send, total):
    _, bit = z_bits()
    total[...] = old[...] + got[...]
    keep[...] = total[rows_at(bit, 48), :]
    send[...] = total[rows_at(1 - bit, 48), :]


def pivot_kernel(widths, weights, pivot, sums, keep, got, block, pay, wide, column):
    g = lax.axis_index("grid")
    kb, k1, k2, a = supers(widths)
    wr, wi = weights[0, 0], weights[0, 1]
    parts = [[sums[GRID_ORDER.index(2 * i + core)] for i in range(8)] for core in range(2)]
    m, t = (functools.reduce(lambda u, v: u + v, part) for part in parts)
    row = iota((32, BIG), 0) + g * 32
    line = iota((32, BIG), 1)
    blank = jnp.zeros((32, HB), F32)
    q = []
    for p in range(2):
        full = jnp.concatenate([u[:, p * HB : (p + 1) * HB] for u in (m, t)], axis=1)
        e = jnp.concatenate([u[:, BIG + p * HS : BIG + (p + 1) * HS] for u in (m, t)], axis=1)
        moved = pltpu.roll(e, HB - a, 1)
        q.append((full, jnp.concatenate([e, blank], axis=1), jnp.concatenate([moved, blank], axis=1)))
    for i, (k, w) in enumerate(((kb, BIG), (k1, a), (k2, HB - a))):
        live = (row < w) & (line < w)
        blocks = []
        for p in range(2):
            b = jnp.where(live, pivot[p, k] - q[p][i], 0.0)
            block[p, k] = b
            blocks.append(b)
        wide[pl.ds(pl.multiple_of(k * 32, 32), 32), :] = wr * blocks[1] + wi * blocks[0]
    d = keep[...] + got[...]
    lane = iota((48, HB), 1)
    small = d[:, BIG:]
    none = jnp.zeros((48, HB), F32)

    def at(k, part):
        return pl.ds(pl.multiple_of(k * BIG + part * HB, HB), HB)

    for part in range(2):
        column[:, at(kb, part)] = d[:, part * HB : (part + 1) * HB]
    column[:, at(k1, 0)] = jnp.where(lane < a, small, 0.0)
    column[:, at(k1, 1)] = none
    column[:, at(k2, 0)] = jnp.where(lane < HB - a, pltpu.roll(small, HB - a, 1), 0.0)
    column[:, at(k2, 1)] = none
    v, w = column[...], wide[...]
    pad = jnp.zeros((16, 32), F32)
    for j, p in enumerate(POLE_ORDER):
        parts = [v[16 * i : 16 * i + 16, 96 * p : 96 * p + 96] for i in range(3)]
        parts += [w[16 * i : 16 * i + 16, 32 * p : 32 * p + 32] for i in range(6)]
        pay[j] = jnp.concatenate(parts + [pad], axis=1)


def density_kernel(pays, column, pivot):
    c = lax.rem(lax.axis_index("grid"), NCORE)
    total = pays[0]
    for p in range(1, 16):
        total = total + pays[p]
    for b0 in range(2):
        for b1 in range(2):
            part = []
            for z in (b0 + 2 * b1, b0 + 2 * b1 + 4):
                for h in range(NH):
                    at = [POLE_ORDER.index((z + core) % NZ * NH + h) for core in range(NCORE)]
                    part.append(pays[jnp.where(c == 0, at[0], at[1])])
            v = (part[0] + part[1]) + (part[2] + part[3])
            for i in range(3):
                row = 96 * b0 + 48 * b1 + 16 * i
                column[row : row + 16] = v[:, 96 * i : 96 * i + 96]
    for i in range(6):
        pivot[i // 2, 16 * (i % 2) : 16 * (i % 2) + 16] = total[:, 288 + 32 * i : 320 + 32 * i]


def local(factor_cols, ancestor_inverse, pivot_inverse, structure, widths, pole_weights):
    structure = structure.T

    def over_grid(v, perm):
        return lax.ppermute(v, "grid", perm)

    block = sds((ROWS, 2 * HC), BF16)
    keep, send = call(
        prep_kernel,
        [block, block],
        [(structure, "p"), (widths, "p"), (factor_cols[0], "p")],
        "prep",
        flops=2 * 2 * ROWS * HB * HB,
        scratch=[
            pltpu.SMEM(structure.shape, jnp.int32),
            pltpu.SMEM(widths.shape, jnp.int32),
            pltpu.VMEM(factor_cols.shape[1:], BF16),
            pltpu.SemaphoreType.DMA((3,)),
        ],
    )
    a_own = ancestor_inverse[0].reshape(2 * ROWS, -1)
    a_sib = over_grid(a_own, CORE)
    got_mine = over_grid(send, CORE)
    got_mine, a_sib = lax.optimization_barrier((got_mine, a_sib))
    got_theirs = over_grid(keep, CORE)

    def first(v):
        return [over_grid(v, perm) for perm in (FROM_AHEAD, FROM_BEHIND, FROM_Y)]

    def second(ahead, behind, beside):
        return [over_grid(ahead, FROM_AHEAD), over_grid(beside, FROM_BEHIND), over_grid(ahead, FROM_Y)]

    def add(old, offsets, us, vs):
        n = len(offsets)
        ins = ([] if old is None else [(old, "v")]) + [(a, "h") for a in (a_own, a_sib)]
        ins += [(b, "h") for b in (*us, *vs)]
        return call(
            functools.partial(acc_kernel, offsets, old is not None),
            [sds((2, ROWS, 2 * HC), F32)],
            ins,
            "product",
            flops=2 * n * 4 * ROWS * 2 * ROWS * 2 * HC,
            scratch=[
                pltpu.VMEM((n, 4 * ROWS, 2 * ROWS), BF16),
                pltpu.VMEM((n, 2 * ROWS, 2 * HC), BF16),
                pltpu.SemaphoreType.DMA((4 * n,)),
            ],
        )[0]

    v1 = first(got_mine)
    u1 = first(keep)
    v2 = second(*v1)
    acc = add(None, [(0, 0)], [keep], [got_mine])
    big, small = call(
        left_kernel,
        [sds((4 * HB, 2 * ROWS), BF16)] * 2,
        [(widths, "s"), (keep, "v"), (send, "v"), (got_mine, "v"), (got_theirs, "v")],
        "left",
        flops=2 * 2 * 2 * ROWS * HB * HB,
    )
    *u1, acc, big, small = lax.optimization_barrier((*u1, acc, big, small))
    u2 = second(*u1)
    acc = add(acc, [(1, 0), (-1, 0), (0, 1)], u1, v1)
    v3 = over_grid(v2[0], FROM_Y)
    *u2, acc = lax.optimization_barrier((*u2, acc))
    u3 = over_grid(u2[1], FROM_BEHIND)
    acc = add(acc, [(2, 0), (-1, 1), (1, 1)], u2, v2)
    own, sib, q = call(
        column_kernel,
        [sds((ROWS, 2 * HC), F32)] * 2 + [sds((16, 32, BIG + HB), F32)],
        [
            (structure, "s"),
            (widths, "s"),
            (acc, "v"),
            (a_own, "h"),
            (a_sib, "h"),
            (u3, "h"),
            (v3, "h"),
            (big, "h"),
            (small, "h"),
        ],
        "column",
        flops=2 * 4 * ROWS * 2 * ROWS * 2 * HC + 2 * 2 * 1024 * 2 * ROWS * 768,
        scratch=[
            pltpu.VMEM((1, 4 * ROWS, 2 * ROWS), BF16),
            pltpu.VMEM((1, 2 * ROWS, 2 * HC), BF16),
            pltpu.VMEM((4 * HB, 2 * ROWS), BF16),
            pltpu.VMEM((4 * HB, 2 * ROWS), BF16),
            pltpu.VMEM((4 * ROWS, 2 * HC), BF16),
            pltpu.VMEM((ROWS, 2 * HC), F32),
            pltpu.VMEM((ROWS, 2 * HC), F32),
            pltpu.VMEM((16, 32, BIG + HB), F32),
            pltpu.SemaphoreType.DMA((4,)),
            pltpu.SemaphoreType.DMA((6,)),
        ],
        limit=20,
        out_space=pltpu.HBM,
    )
    other = over_grid(sib, CORE)
    sums = lax.all_to_all(q, "grid", 0, 0, axis_index_groups=[GRID_ORDER], tiled=True)
    d_keep, d_send = call(
        term_kernel,
        [sds((96, 768), F32)] * 2,
        [(pole_weights, "s"), (own, "v"), (other, "v")],
        "term",
        scratch=[pltpu.VMEM((ROWS, 768), F32)],
    )
    d_got = lax.ppermute(d_send, ("pole", "grid"), z_pair(1))
    column_inverse = call(
        spread_kernel,
        [sds((2, ROWS, 3 * BIG), BF16)],
        [(widths, "s"), (own, "v"), (other, "v")],
        "spread",
    )[0]
    d_got, column_inverse = lax.optimization_barrier((d_got, column_inverse))
    d_keep, d_send = call(
        second_kernel,
        [sds((48, 768), F32)] * 2,
        [(d_keep, "v"), (d_got, "v")],
        "second",
        scratch=[pltpu.VMEM((96, 768), F32)],
    )
    d_got = lax.ppermute(d_send, ("pole", "grid"), z_pair(2))
    sums, d_keep = lax.optimization_barrier((sums, d_keep))
    pivot_block, pay = call(
        pivot_kernel,
        [sds((2, 3, 32, BIG), F32), sds((16, 16, 512), F32)],
        [
            (widths, "s"),
            (pole_weights, "s"),
            (pivot_inverse[0], "v"),
            (sums, "v"),
            (d_keep, "v"),
            (d_got, "v"),
        ],
        "pivot",
        scratch=[pltpu.VMEM((96, BIG), F32), pltpu.VMEM((48, 3 * BIG), F32)],
    )
    pays = lax.all_to_all(pay, "pole", 0, 0, axis_index_groups=[POLE_ORDER], tiled=True)
    density_column, density_pivot = call(
        density_kernel, [sds((ROWS, 96), F32), sds((3, 32, 32), F32)], [(pays, "v")], "density"
    )
    return (column_inverse[None], pivot_block[None], density_column, density_pivot)


def solution(mesh):
    in_specs = (
        P("pole", None, "grid", None),
        P("pole", None, "grid", None),
        P("pole", None, None, "grid", None),
        P(),
        P(),
        P("pole", None),
    )
    out_specs = (
        P("pole", None, "grid", None),
        P("pole", None, None, "grid", None),
        P("grid", "pole"),
        P(None, "grid", "pole"),
    )
    return jax.shard_map(local, mesh=mesh, in_specs=in_specs, out_specs=out_specs, check_vma=False)
```

```python
import functools

import jax
import jax.numpy as jnp
from jax import lax
from jax.experimental import pallas as pl
from jax.experimental.pallas import tpu as pltpu
from jax.sharding import PartitionSpec as P

F32 = jnp.float32
BF16 = jnp.bfloat16
BIG = 512
ROWS = 192
HB = 256
HS = 128
HC = HB + HS

NX, NY, NCORE = 4, 2, 2
NZ, NH = 8, 2


def grid_perm(source):
    def at(y, x, c):
        return (y * NX + x % NX) * NCORE + c

    return [
        (at(*source(y, x, c)), at(y, x, c)) for y in range(NY) for x in range(NX) for c in range(NCORE)
    ]


CORE = grid_perm(lambda y, x, c: (y, x, 1 - c))
FROM_AHEAD = grid_perm(lambda y, x, c: (y, x + 1 - 2 * c, c))
FROM_BEHIND = grid_perm(lambda y, x, c: (y, x - 1 + 2 * c, c))
FROM_FAR = grid_perm(lambda y, x, c: (y, x + 2, c))
FROM_Y = grid_perm(lambda y, x, c: (1 - y, x, c))


def z_pair(bit):
    def at(z, h, g):
        return ((z % NZ) * NH + h) * NX * NY * NCORE + g

    return [
        (at((((z - g % NCORE) % NZ) ^ bit) + g % NCORE, h, g), at(z, h, g))
        for z in range(NZ)
        for h in range(NH)
        for g in range(NX * NY * NCORE)
    ]


POLE_ORDER = [z * NH + h for z in (0, 7, 2, 5, 1, 6, 3, 4) for h in range(NH)]
GRID_ORDER = [(y * NX + x) * NCORE + c for x in (0, 2, 1, 3) for y in range(NY) for c in range(NCORE)]


def place():
    g = lax.axis_index("grid")
    c = lax.rem(g, 2)
    x = lax.rem(lax.div(g, 2), NX)
    y = lax.div(g, 2 * NX)
    return g, c, x, y


def z_bits():
    z = lax.div(lax.axis_index("pole"), NH)
    z = lax.rem(z + NZ - lax.rem(lax.axis_index("grid"), NCORE), NZ)
    return lax.rem(z, 2), lax.rem(lax.div(z, 2), 2)


def supers(widths):
    kb = jnp.where(widths[0] == BIG, 0, jnp.where(widths[1] == BIG, 1, 2))
    k1 = jnp.where(kb == 0, 1, 0)
    k2 = jnp.where(kb == 2, 1, 2)
    return kb, k1, k2, widths[k1]


def iota(shape, axis):
    return lax.broadcasted_iota(jnp.int32, shape, axis)


def row_mask(structure, block, count, k, lanes):
    return jnp.concatenate(
        [jnp.full((32, lanes), structure[k, block + i].astype(F32), F32) for i in range(count)], axis=0
    )


def call(body, outs, ins, name, flops=0, scratch=(), limit=16, out_space=pltpu.VMEM):
    spaces = {"s": pltpu.SMEM, "v": pltpu.VMEM, "h": pltpu.HBM, "p": pltpu.HBM}
    size = sum(a.size * a.dtype.itemsize for a, _ in ins) + sum(
        o.size * o.dtype.itemsize for o in outs
    )
    if out_space is pltpu.HBM:
        outs = [pltpu.HBM(o.shape, o.dtype) for o in outs]
    return pl.pallas_call(
        body,
        out_shape=tuple(outs),
        in_specs=[pl.BlockSpec(memory_space=spaces[kind]) for _, kind in ins],
        out_specs=tuple(pl.BlockSpec(memory_space=out_space) for _ in outs),
        scratch_shapes=list(scratch),
        compiler_params=pltpu.CompilerParams(vmem_limit_bytes=limit * 1024 * 1024),
        cost_estimate=pl.CostEstimate(flops=flops, bytes_accessed=size, transcendentals=0),
        name=name,
    )(*[pltpu.with_memory_space_constraint(a, pltpu.HBM) if kind == "p" else a for a, kind in ins])


def sds(shape, dtype):
    return jax.ShapeDtypeStruct(shape, dtype)


def prep_kernel(structure_in, widths_in, f_in, keep, send, structure, widths, f, sems):
    pairs = ((widths_in, widths), (structure_in, structure), (f_in, f))
    copies = [pltpu.make_async_copy(v, to, sems.at[i]) for i, (v, to) in enumerate(pairs)]
    for copy in copies:
        copy.start()
    for copy in copies:
        copy.wait()
    g, c, _, _ = place()
    kb, k1, k2, a = supers(widths)
    base = g * 6
    mask_b = row_mask(structure, base, 6, kb, HB).astype(BF16)
    mask_1 = row_mask(structure, base, 6, k1, HB).astype(BF16)
    mask_2 = row_mask(structure, base, 6, k2, HB).astype(BF16)
    shift = (iota((HB, HB), 0) + a == iota((HB, HB), 1)).astype(BF16)
    first = iota((ROWS, HB), 1) < a

    def at(k, part):
        return pl.ds(pl.multiple_of(k * BIG + part * HB, HB), HB)

    for p in range(2):
        o = p * HC
        keep[:, o : o + HB] = f[p, :, at(kb, c)] * mask_b
        send[:, o : o + HB] = f[p, :, at(kb, 1 - c)] * mask_b
        one = (f[p, :, at(k1, 0)] * mask_1).astype(F32)
        two = jnp.dot(f[p, :, at(k2, 0)] * mask_2, shift, preferred_element_type=F32)
        small = jnp.where(first, one, two)
        low, high = small[:, :HS], small[:, HS:]
        keep[:, o + HB : o + HC] = jnp.where(c == 0, low, high).astype(BF16)
        send[:, o + HB : o + HC] = jnp.where(c == 0, high, low).astype(BF16)


def left_kernel(widths, keep, send, got_mine, got_theirs, big, small):
    _, c, _, _ = place()
    _, _, _, a = supers(widths)
    back = (iota((HB, HB), 0) == iota((HB, HB), 1) + a).astype(BF16)
    mine = jnp.concatenate([keep[...], got_mine[...]], axis=0)
    theirs = jnp.concatenate([send[...], got_theirs[...]], axis=0)
    for p in range(2):
        o = p * HC
        for part, half in ((c, mine), (1 - c, theirs)):
            at = pl.ds(pl.multiple_of((2 * part + p) * HB, HB), HB)
            big[at, :] = half[:, o : o + HB].astype(F32).T.astype(BF16)
        m, t = mine[:, o + HB : o + HC].astype(F32), theirs[:, o + HB : o + HC].astype(F32)
        low, high = jnp.where(c == 0, m, t), jnp.where(c == 0, t, m)
        both = jnp.concatenate([low, high], axis=1)
        moved = jnp.dot(both.astype(BF16), back, preferred_element_type=F32)
        small[p * HB : (p + 1) * HB] = both.T.astype(BF16)
        small[(2 + p) * HB : (3 + p) * HB] = moved.T.astype(BF16)


def rows_at(bit, count):
    return pl.ds(pl.multiple_of(bit * count, count), count)


def block_copies(offsets, a_own, a_sib, us, vs, left, rows, sems):
    _, c, x, y = place()
    side = 1 - 2 * c
    copies = []
    for i, (dx, dy) in enumerate(offsets):
        at = lax.rem(y + dy, NY) * NX + lax.rem(x + dx * side + NX, NX)
        cols = pl.ds(pl.multiple_of(at * 2 * ROWS, 2 * ROWS), 2 * ROWS)
        pairs = [
            (us[i], rows.at[i, rows_at(c, ROWS)]),
            (vs[i], rows.at[i, rows_at(1 - c, ROWS)]),
            (a_own.at[:, cols], left.at[i, : 2 * ROWS]),
            (a_sib.at[:, cols], left.at[i, 2 * ROWS :]),
        ]
        copies += [pltpu.make_async_copy(v, to, sems.at[4 * i + j]) for j, (v, to) in enumerate(pairs)]
    return copies


def add_blocks(copies, left, rows, get, put):
    z = None
    for i in range(len(copies) // 4):
        for copy in copies[4 * i : 4 * i + 4]:
            copy.wait()
        d = jnp.dot(left[i], rows[i], preferred_element_type=F32)
        z = d if z is None else z + d
    for s in range(2):
        re, im = z[2 * s * ROWS : (2 * s + 1) * ROWS], z[(2 * s + 1) * ROWS : (2 * s + 2) * ROWS]
        old_re, old_im = get(s)
        put(s, old_re + (re[:, :HC] - im[:, HC:]), old_im + (re[:, HC:] + im[:, :HC]))


def acc_kernel(offsets, has_acc, *refs):
    refs = list(refs)
    old = refs.pop(0) if has_acc else None
    n = len(offsets)
    a_own, a_sib, us, vs = refs[0], refs[1], refs[2 : 2 + n], refs[2 + n : 2 + 2 * n]
    out, left, rows, sems = refs[2 + 2 * n :]
    copies = block_copies(offsets, a_own, a_sib, us, vs, left, rows, sems)
    for copy in copies:
        copy.start()

    def get(s):
        if old is None:
            return 0.0, 0.0
        return old[s, :, :HC], old[s, :, HC:]

    def put(s, re, im):
        out[s, :, :HC] = re
        out[s, :, HC:] = im

    add_blocks(copies, left, rows, get, put)


def column_kernel(structure, widths, old, a_own, a_sib, u, v, big_in, small_in, own_out, sib_out, q_out, *scratch):
    left, rows, big, small, gs, own, sib, q, sems, in_sems = scratch
    g, c, _, _ = place()
    kb, k1, k2, a = supers(widths)

    def get(s):
        return old[s, :, :HC], old[s, :, HC:]

    def put(s, re, im):
        base = (g + s * (1 - 2 * c)) * 6
        mask_b = row_mask(structure, base, 6, kb, HB)
        mask_1 = row_mask(structure, base, 6, k1, HS)
        mask_2 = row_mask(structure, base, 6, k2, HS)
        mask_s = jnp.where(iota((ROWS, HS), 1) + c * HS < a, mask_1, mask_2)
        out = own if s == 0 else sib
        for p, w in ((0, re), (1, im)):
            vb = -(w[:, :HB] * mask_b)
            vs = -(w[:, HB:] * mask_s)
            out[:, p * HC : p * HC + HB] = vb
            out[:, p * HC + HB : (p + 1) * HC] = vs
            for part, lo, hi in ((vb, p * HB, (p + 1) * HB), (vs, 2 * HB + p * HS, 2 * HB + (p + 1) * HS)):
                top = part.astype(BF16)
                gs[s * ROWS : (s + 1) * ROWS, lo:hi] = top
                gs[(s + 2) * ROWS : (s + 3) * ROWS, lo:hi] = (part - top.astype(F32)).astype(BF16)

    blocks = block_copies([(2, 1)], a_own, a_sib, [u], [v], left, rows, in_sems)
    lefts = [
        pltpu.make_async_copy(big_in, big, in_sems.at[4]),
        pltpu.make_async_copy(small_in, small, in_sems.at[5]),
    ]
    for copy in blocks + lefts:
        copy.start()
    add_blocks(blocks, left, rows, get, put)
    copies = [pltpu.make_async_copy(sib, sib_out, sems.at[0]), pltpu.make_async_copy(own, own_out, sems.at[1])]
    for copy in copies:
        copy.start()

    def across(left, lo, hi):
        twice = jnp.concatenate([left[...], left[...]], axis=1)
        return jnp.dot(twice, gs[:, lo:hi], preferred_element_type=F32)

    lefts[0].wait()
    z = across(big, 0, BIG)
    for h in range(2):
        re, im = z[2 * h * HB : (2 * h + 1) * HB], z[(2 * h + 1) * HB : (2 * h + 2) * HB]
        for t in range(8):
            r = slice(32 * t, 32 * t + 32)
            to = GRID_ORDER.index(8 * h + t)
            q[to, :, :HB] = re[r, :HB] - im[r, HB:]
            q[to, :, HB:BIG] = re[r, HB:] + im[r, :HB]
    copies.append(pltpu.make_async_copy(q.at[:, :, :BIG], q_out.at[:, :, :BIG], sems.at[2]))
    copies[2].start()
    lefts[1].wait()
    z = across(small, BIG, BIG + HB)
    col = iota((HB, HS), 1) + c * HS
    row = iota((HB, HS), 0)
    parts = []
    for i in range(2):
        re, im = z[2 * i * HB : (2 * i + 1) * HB], z[(2 * i + 1) * HB : (2 * i + 2) * HB]
        parts.append((re[:, :HS] - im[:, HS:], re[:, HS:] + im[:, :HS]))
    for p in range(2):
        e = jnp.where(
            col < a, jnp.where(row < a, parts[0][p], 0.0), jnp.where(row < HB - a, parts[1][p], 0.0)
        )
        at = slice(BIG + p * HS, BIG + (p + 1) * HS)
        for t in range(8):
            q[GRID_ORDER.index(t), :, at] = e[32 * t : 32 * t + 32]
            q[GRID_ORDER.index(8 + t), :, at] = jnp.zeros((32, HS), F32)
    copies.append(pltpu.make_async_copy(q.at[:, :, BIG:], q_out.at[:, :, BIG:], sems.at[3]))
    copies[3].start()
    for copy in copies:
        copy.wait()


def halves_of(mine, other):
    return [
        [(ref[:, p * HC : p * HC + HB], ref[:, p * HC + HB : (p + 1) * HC]) for p in range(2)]
        for ref in (mine, other)
    ]


def in_order(c, first, second):
    return jnp.concatenate([jnp.where(c == 0, first, second), jnp.where(c == 0, second, first)], axis=1)


def term_kernel(weights, mine, other, keep, send, wide):
    _, c, _, _ = place()
    odd, _ = z_bits()
    wr, wi = weights[0, 0], weights[0, 1]
    m, t = ([wr * half[1][i] + wi * half[0][i] for i in range(2)] for half in halves_of(mine, other))
    wide[:, :BIG] = in_order(c, m[0], t[0])
    wide[:, BIG:] = in_order(c, m[1], t[1])
    keep[...] = wide[rows_at(odd, 96), :]
    send[...] = wide[rows_at(1 - odd, 96), :]


def spread_kernel(widths, mine, other, out):
    _, c, _, _ = place()
    kb, k1, k2, a = supers(widths)
    back = (iota((HB, HB), 0) == iota((HB, HB), 1) + a).astype(BF16)
    lane = iota((ROWS, HB), 1)

    def at(k, part):
        return pl.ds(pl.multiple_of(k * BIG + part * HB, HB), HB)

    zero = jnp.zeros((ROWS, HB), BF16)
    halves = halves_of(mine, other)
    for p in range(2):
        m, t = halves[0][p], halves[1][p]
        out[p, :, at(kb, c)] = m[0].astype(BF16)
        out[p, :, at(kb, 1 - c)] = t[0].astype(BF16)
        s = in_order(c, m[1], t[1])
        out[p, :, at(k1, 0)] = jnp.where(lane < a, s, 0.0).astype(BF16)
        out[p, :, at(k1, 1)] = zero
        out[p, :, at(k2, 0)] = jnp.dot(s.astype(BF16), back, preferred_element_type=F32).astype(BF16)
        out[p, :, at(k2, 1)] = zero


def second_kernel(old, got, keep, send, total):
    _, bit = z_bits()
    total[...] = old[...] + got[...]
    keep[...] = total[rows_at(bit, 48), :]
    send[...] = total[rows_at(1 - bit, 48), :]


def pivot_kernel(widths, weights, pivot, sums, keep, got, block, pay, wide, column):
    g = lax.axis_index("grid")
    kb, k1, k2, a = supers(widths)
    wr, wi = weights[0, 0], weights[0, 1]
    parts = [[sums[GRID_ORDER.index(2 * i + core)] for i in range(8)] for core in range(2)]
    m, t = (functools.reduce(lambda u, v: u + v, part) for part in parts)
    row = iota((32, BIG), 0) + g * 32
    line = iota((32, BIG), 1)
    blank = jnp.zeros((32, HB), F32)
    q = []
    for p in range(2):
        full = jnp.concatenate([u[:, p * HB : (p + 1) * HB] for u in (m, t)], axis=1)
        e = jnp.concatenate([u[:, BIG + p * HS : BIG + (p + 1) * HS] for u in (m, t)], axis=1)
        moved = pltpu.roll(e, HB - a, 1)
        q.append((full, jnp.concatenate([e, blank], axis=1), jnp.concatenate([moved, blank], axis=1)))
    for i, (k, w) in enumerate(((kb, BIG), (k1, a), (k2, HB - a))):
        live = (row < w) & (line < w)
        blocks = []
        for p in range(2):
            b = jnp.where(live, pivot[p, k] - q[p][i], 0.0)
            block[p, k] = b
            blocks.append(b)
        wide[pl.ds(pl.multiple_of(k * 32, 32), 32), :] = wr * blocks[1] + wi * blocks[0]
    d = keep[...] + got[...]
    lane = iota((48, HB), 1)
    small = d[:, BIG:]
    none = jnp.zeros((48, HB), F32)

    def at(k, part):
        return pl.ds(pl.multiple_of(k * BIG + part * HB, HB), HB)

    for part in range(2):
        column[:, at(kb, part)] = d[:, part * HB : (part + 1) * HB]
    column[:, at(k1, 0)] = jnp.where(lane < a, small, 0.0)
    column[:, at(k1, 1)] = none
    column[:, at(k2, 0)] = jnp.where(lane < HB - a, pltpu.roll(small, HB - a, 1), 0.0)
    column[:, at(k2, 1)] = none
    v, w = column[...], wide[...]
    pad = jnp.zeros((16, 32), F32)
    for j, p in enumerate(POLE_ORDER):
        parts = [v[16 * i : 16 * i + 16, 96 * p : 96 * p + 96] for i in range(3)]
        parts += [w[16 * i : 16 * i + 16, 32 * p : 32 * p + 32] for i in range(6)]
        pay[j] = jnp.concatenate(parts + [pad], axis=1)


def density_kernel(pays, column, pivot):
    c = lax.rem(lax.axis_index("grid"), NCORE)
    total = pays[0]
    for p in range(1, 16):
        total = total + pays[p]
    for b0 in range(2):
        for b1 in range(2):
            part = []
            for z in (b0 + 2 * b1, b0 + 2 * b1 + 4):
                for h in range(NH):
                    at = [POLE_ORDER.index((z + core) % NZ * NH + h) for core in range(NCORE)]
                    part.append(pays[jnp.where(c == 0, at[0], at[1])])
            v = (part[0] + part[1]) + (part[2] + part[3])
            for i in range(3):
                row = 96 * b0 + 48 * b1 + 16 * i
                column[row : row + 16] = v[:, 96 * i : 96 * i + 96]
    for i in range(6):
        pivot[i // 2, 16 * (i % 2) : 16 * (i % 2) + 16] = total[:, 288 + 32 * i : 320 + 32 * i]


def local(factor_cols, ancestor_inverse, pivot_inverse, structure, widths, pole_weights):
    structure = structure.T

    def over_grid(v, perm):
        return lax.ppermute(v, "grid", perm)

    block = sds((ROWS, 2 * HC), BF16)
    keep, send = call(
        prep_kernel,
        [block, block],
        [(structure, "p"), (widths, "p"), (factor_cols[0], "p")],
        "prep",
        flops=2 * 2 * ROWS * HB * HB,
        scratch=[
            pltpu.SMEM(structure.shape, jnp.int32),
            pltpu.SMEM(widths.shape, jnp.int32),
            pltpu.VMEM(factor_cols.shape[1:], BF16),
            pltpu.SemaphoreType.DMA((3,)),
        ],
    )
    a_own = ancestor_inverse[0].reshape(2 * ROWS, -1)
    a_sib = over_grid(a_own, CORE)
    got_mine = over_grid(send, CORE)
    got_mine, a_sib = lax.optimization_barrier((got_mine, a_sib))
    got_theirs = over_grid(keep, CORE)

    def first(v):
        return [over_grid(v, perm) for perm in (FROM_AHEAD, FROM_BEHIND, FROM_Y)]

    def second(ahead, behind, beside):
        return [over_grid(ahead, FROM_AHEAD), over_grid(beside, FROM_BEHIND), over_grid(ahead, FROM_Y)]

    def add(old, offsets, us, vs):
        n = len(offsets)
        ins = ([] if old is None else [(old, "v")]) + [(a, "h") for a in (a_own, a_sib)]
        ins += [(b, "h") for b in (*us, *vs)]
        return call(
            functools.partial(acc_kernel, offsets, old is not None),
            [sds((2, ROWS, 2 * HC), F32)],
            ins,
            "product",
            flops=2 * n * 4 * ROWS * 2 * ROWS * 2 * HC,
            scratch=[
                pltpu.VMEM((n, 4 * ROWS, 2 * ROWS), BF16),
                pltpu.VMEM((n, 2 * ROWS, 2 * HC), BF16),
                pltpu.SemaphoreType.DMA((4 * n,)),
            ],
        )[0]

    v1 = first(got_mine)
    u1 = first(keep)
    v2 = second(*v1)
    acc = add(None, [(0, 0)], [keep], [got_mine])
    big, small = call(
        left_kernel,
        [sds((4 * HB, 2 * ROWS), BF16)] * 2,
        [(widths, "s"), (keep, "v"), (send, "v"), (got_mine, "v"), (got_theirs, "v")],
        "left",
        flops=2 * 2 * 2 * ROWS * HB * HB,
    )
    *u1, acc, big, small = lax.optimization_barrier((*u1, acc, big, small))
    u2 = second(*u1)
    acc = add(acc, [(1, 0), (-1, 0), (0, 1)], u1, v1)
    v3 = over_grid(v2[0], FROM_Y)
    *u2, acc = lax.optimization_barrier((*u2, acc))
    u3 = over_grid(u2[1], FROM_BEHIND)
    acc = add(acc, [(2, 0), (-1, 1), (1, 1)], u2, v2)
    own, sib, q = call(
        column_kernel,
        [sds((ROWS, 2 * HC), F32)] * 2 + [sds((16, 32, BIG + HB), F32)],
        [
            (structure, "s"),
            (widths, "s"),
            (acc, "v"),
            (a_own, "h"),
            (a_sib, "h"),
            (u3, "h"),
            (v3, "h"),
            (big, "h"),
            (small, "h"),
        ],
        "column",
        flops=2 * 4 * ROWS * 2 * ROWS * 2 * HC + 2 * 2 * 1024 * 2 * ROWS * 768,
        scratch=[
            pltpu.VMEM((1, 4 * ROWS, 2 * ROWS), BF16),
            pltpu.VMEM((1, 2 * ROWS, 2 * HC), BF16),
            pltpu.VMEM((4 * HB, 2 * ROWS), BF16),
            pltpu.VMEM((4 * HB, 2 * ROWS), BF16),
            pltpu.VMEM((4 * ROWS, 2 * HC), BF16),
            pltpu.VMEM((ROWS, 2 * HC), F32),
            pltpu.VMEM((ROWS, 2 * HC), F32),
            pltpu.VMEM((16, 32, BIG + HB), F32),
            pltpu.SemaphoreType.DMA((4,)),
            pltpu.SemaphoreType.DMA((6,)),
        ],
        limit=20,
        out_space=pltpu.HBM,
    )
    other = over_grid(sib, CORE)
    sums = lax.all_to_all(q, "grid", 0, 0, axis_index_groups=[GRID_ORDER], tiled=True)
    d_keep, d_send = call(
        term_kernel,
        [sds((96, 768), F32)] * 2,
        [(pole_weights, "s"), (own, "v"), (other, "v")],
        "term",
        scratch=[pltpu.VMEM((ROWS, 768), F32)],
    )
    d_got = lax.ppermute(d_send, ("pole", "grid"), z_pair(1))
    column_inverse = call(
        spread_kernel,
        [sds((2, ROWS, 3 * BIG), BF16)],
        [(widths, "s"), (own, "v"), (other, "v")],
        "spread",
    )[0]
    d_got, column_inverse = lax.optimization_barrier((d_got, column_inverse))
    d_keep, d_send = call(
        second_kernel,
        [sds((48, 768), F32)] * 2,
        [(d_keep, "v"), (d_got, "v")],
        "second",
        scratch=[pltpu.VMEM((96, 768), F32)],
    )
    d_got = lax.ppermute(d_send, ("pole", "grid"), z_pair(2))
    sums, d_keep = lax.optimization_barrier((sums, d_keep))
    pivot_block, pay = call(
        pivot_kernel,
        [sds((2, 3, 32, BIG), F32), sds((16, 16, 512), F32)],
        [
            (widths, "s"),
            (pole_weights, "s"),
            (pivot_inverse[0], "v"),
            (sums, "v"),
            (d_keep, "v"),
            (d_got, "v"),
        ],
        "pivot",
        scratch=[pltpu.VMEM((96, BIG), F32), pltpu.VMEM((48, 3 * BIG), F32)],
    )
    pays = lax.all_to_all(pay, "pole", 0, 0, axis_index_groups=[POLE_ORDER], tiled=True)
    density_column, density_pivot = call(
        density_kernel, [sds((ROWS, 96), F32), sds((3, 32, 32), F32)], [(pays, "v")], "density"
    )
    return (column_inverse[None], pivot_block[None], density_column, density_pivot)


def solution(mesh):
    in_specs = (
        P("pole", None, "grid", None),
        P("pole", None, "grid", None),
        P("pole", None, None, "grid", None),
        P(),
        P(),
        P("pole", None),
    )
    out_specs = (
        P("pole", None, "grid", None),
        P("pole", None, None, "grid", None),
        P("grid", "pole"),
        P(None, "grid", "pole"),
    )
    return jax.shard_map(local, mesh=mesh, in_specs=in_specs, out_specs=out_specs, check_vma=False)
```
